128 devices in a mesh: mem: 16 (over y, x), reg: 8 (over z, core).
Axes of the slice: x: 4, y: 4, z: 4, core: 2. Of those that a mesh axis runs over, the one named last changes fastest.
Arguments:
- prior_samples: bfloat16 [1024, 16, 8, 1920], P('mem', None, 'reg'), may hold values from -7 to 7
- measured_anomalies: bfloat16 [16, 8, 2048, 1024], P('mem', 'reg'), may hold values from -6 to 6
- measured_departure: bfloat16 [16, 8, 2048], P('mem', 'reg'), may hold values from -6 to 6
- measure_inverse_variance: bfloat16 [16, 8, 2048], P('mem', 'reg'), may hold values from 0.25 to 4
- measure_neighbour_code: int32 [16, 8, 2560], P('mem', 'reg'), may hold values from 0 to 2
- measure_position: int32 [16, 8, 2560], P('mem', 'reg'), may hold values from 0 to 2047, as said below
- measure_tally: int32 [16, 8], P('mem', 'reg'), may hold values from 1280 to 2560, as said below
- locality_weights: float32 [16, 8, 2560], P('mem', 'reg'), may hold values from 0.1 to 1
Outputs:
- analysis: bfloat16 [1024, 16, 8, 1920], P('mem', None, 'reg')
The draws below stay inside these ranges and needn't reach their ends.
Inputs may be any that keep to these rules, and one draw needn't show every extreme that they name: `measure_position`: an entry with measure_neighbour_code 0 names one of the last 512 rows of its block, one with measure_neighbour_code 2 one of the first 512; the 2560 entries of one block's list name distinct observations. `measure_tally`: some block uses all 2560 entries and some block exactly 1280.
All inputs are finite; a program needn't handle non-finite values.
Results may differ from the reference program's by a relative error of at most 0.0017.
The reference program's roundings to bfloat16 on the way count: a program that leaves them out, or rounds other values in their place, can miss the bound.
Values may be sent and summed in bfloat16 or wider, within the bound.
A program may use at most 128 MiB of HBM per device.

```python
import math
import jax
import jax.numpy as jnp
from jax import lax

K = 1024
OWN = 2048
GRID_POINTS_EACH = 1920
RIM = 512
LOC = 2560
BOUTER = 16
BINNER = 8


def pool_lists(key):
    pool_size = OWN + 2 * RIM

    def single_list(sub_key):
        middle = jax.random.permutation(sub_key, jnp.arange(1, pool_size - 1, dtype=jnp.int32))[:LOC - 2]
        chosen = jnp.concatenate([jnp.array([0, pool_size - 1], dtype=jnp.int32), middle])
        shuffle = jax.random.permutation(jax.random.fold_in(sub_key, 7), LOC)
        return chosen[shuffle]
    pool_ids = jax.vmap(single_list)(jax.random.split(key, BOUTER * BINNER)).reshape(BOUTER, BINNER, LOC)
    side_code = jnp.where(pool_ids < RIM, 0, jnp.where(pool_ids < RIM + OWN, 1, 2)).astype(jnp.int32)
    slot_code = jnp.where(side_code == 0, pool_ids + OWN - RIM, jnp.where(side_code == 1, pool_ids - RIM, pool_ids - RIM - OWN)).astype(jnp.int32)
    return (side_code, slot_code)


def draw_measure_neighbour_code(key, part):
    side_code, slot_code = pool_lists(key)
    return side_code


def draw_measure_position(key, part):
    side_code, slot_code = pool_lists(key)
    return slot_code


def draw_measure_tally(key, part):
    key = jax.random.fold_in(key, 11)
    first_key, second_key, third_key = jax.random.split(key, 3)
    block_total = BOUTER * BINNER
    counts = jax.random.randint(first_key, (block_total,), LOC // 2, LOC + 1)
    full_block = jax.random.randint(second_key, (), 0, block_total)
    half_block = (full_block + 1 + jax.random.randint(third_key, (), 0, block_total - 1)) % block_total
    places = jnp.arange(block_total)
    counts = jnp.where(places == full_block, LOC, jnp.where(places == half_block, LOC // 2, counts))
    return counts.reshape(BOUTER, BINNER).astype(jnp.int32)


def draw_prior_samples(key, part):
    key = jax.random.fold_in(key, 5)
    mean_key, member_key = jax.random.split(key)
    full_shape = (K, BOUTER, BINNER, GRID_POINTS_EACH)
    mean_field = jnp.clip(jax.random.normal(mean_key, (1, BOUTER, BINNER, GRID_POINTS_EACH), jnp.float32), -3.0, 3.0)
    member_part = jnp.clip(jax.random.normal(member_key, full_shape, jnp.float32), -4.0, 4.0)
    return (mean_field + member_part).astype(jnp.bfloat16)


def block_levels(own_key, dims, cuts, least, top_value):
    level, own = 1.0, jax.random.fold_in(own_key, 6)
    for dim, blocks in cuts:
        steps = jnp.exp(jax.random.uniform(jax.random.fold_in(own, dim), (blocks,), jnp.float32, least / len(cuts), top_value / len(cuts)))
        level = level * jnp.repeat(steps, dims[dim] // blocks).reshape([-1 if axis == dim else 1 for axis in range(len(dims))])
    return level


def centred(key, dims, scale, most, cuts=(), kind=jnp.bfloat16):
    result = scale * jax.random.normal(key, dims, jnp.float32)
    if cuts:
        result = result * block_levels(key, dims, cuts, -0.22, 0.18)
    return jnp.clip(result, -most, most).astype(kind)


def setup_inputs(seed: int = 0) -> dict:
    key_list = jax.random.split(jax.random.key(seed), 9)
    return {
        "prior_samples": draw_prior_samples(jax.random.fold_in(key_list[8], 71), 0),
        "measured_anomalies": centred(key_list[1], (BOUTER, BINNER, OWN, K), 1.0, 6.0, ((0, 16), (1, 8))),
        "measured_departure": centred(key_list[2], (BOUTER, BINNER, OWN), 1.0, 6.0, ((0, 16), (1, 8))),
        "measure_inverse_variance": jnp.clip(jnp.exp(math.log(4.0) - 2.7725887 * jax.random.uniform(key_list[3], (BOUTER, BINNER, OWN), jnp.float32) ** block_levels(key_list[3], (BOUTER, BINNER, OWN), ((0, 16), (1, 8)), -0.2, 0.2)), 0.25, 4.0).astype(jnp.bfloat16),
        "measure_neighbour_code": draw_measure_neighbour_code(jax.random.fold_in(key_list[8], 71), 0),
        "measure_position": draw_measure_position(jax.random.fold_in(key_list[8], 71), 0),
        "measure_tally": draw_measure_tally(jax.random.fold_in(key_list[8], 71), 0),
        "locality_weights": jnp.clip(0.1 + 0.9 * jax.random.uniform(key_list[7], (BOUTER, BINNER, LOC), jnp.float32) ** block_levels(key_list[7], (BOUTER, BINNER, LOC), ((0, 16), (1, 8)), -0.2, 0.2), 0.1, 1.0),
    }


inflation = 1.1

def top_dot(left, right):
    return jnp.dot(left, right, precision=lax.Precision.HIGHEST)

def transform_matrix(picked, weight, innov_picked):
    sample_total = picked.shape[1]
    scaled = (picked.astype(jnp.float32) * weight[:, None]).astype(jnp.bfloat16)
    gram_matrix = lax.dot_general(scaled, picked, (((0,), (0,)), ((), ())), preferred_element_type=jnp.float32)
    forcing = (weight * innov_picked).astype(jnp.bfloat16)
    drive_vec = jnp.dot(forcing, picked, preferred_element_type=jnp.float32)
    identity = jnp.eye(sample_total, dtype=jnp.float32)
    system = gram_matrix + (sample_total - 1) / inflation * identity
    probe_vec = jnp.ones((sample_total,), jnp.float32)
    for iteration in range(6):
        probe_vec = top_dot(system, probe_vec)
        probe_vec = probe_vec / jnp.sqrt(jnp.sum(probe_vec * probe_vec))
    bound_val = jnp.sum(probe_vec * top_dot(system, probe_vec))
    unit_sys = system / bound_val
    first_step = (3.0 * identity - unit_sys) * 0.5
    second = (3.0 * identity - top_dot(first_step, top_dot(unit_sys, first_step))) * 0.5
    root_inv = top_dot(second, first_step)
    mean_weights = top_dot(root_inv, top_dot(root_inv, drive_vec)) / bound_val
    return (jnp.sqrt((sample_total - 1) / bound_val) * root_inv + mean_weights[:, None]).astype(jnp.bfloat16)

def apply_transform(ensemble_transform, grid_width):
    sample_total = grid_width.shape[0]
    center = lax.optimization_barrier(jnp.sum(grid_width, axis=0, dtype=jnp.float32)) / sample_total
    deviation = (grid_width.astype(jnp.float32) - center).astype(jnp.bfloat16)
    moved = lax.dot_general(ensemble_transform, deviation, (((0,), (0,)), ((), ())), preferred_element_type=jnp.float32)
    return (center + moved).astype(jnp.bfloat16)

def reference(prior_samples, measured_anomalies, measured_departure, measure_inverse_variance, measure_neighbour_code, measure_position, measure_tally, locality_weights):
    segment_total = BOUTER * BINNER
    sample_total = prior_samples.shape[0]
    prior_lines_serial = prior_samples.reshape(sample_total, segment_total, GRID_POINTS_EACH)
    obs_flat = measured_anomalies.reshape(segment_total, OWN, sample_total)
    innov_flat = measured_departure.reshape(segment_total, OWN)
    prec_flat = measure_inverse_variance.reshape(segment_total, OWN)
    side_flat = measure_neighbour_code.reshape(segment_total, LOC)
    slot_flat = measure_position.reshape(segment_total, LOC)
    count_flat = measure_tally.reshape(segment_total)
    taper_flat = locality_weights.reshape(segment_total, LOC)

    def one_block(segment_index):
        before_id = (segment_index + segment_total - 1) % segment_total
        after_id = (segment_index + 1) % segment_total

        def neighbours(table):
            return jnp.concatenate([table[before_id], table[segment_index], table[after_id]], axis=0)
        window_rows = neighbours(obs_flat)
        window_innov = neighbours(innov_flat)
        window_prec = neighbours(prec_flat)
        window_index = (side_flat[segment_index] * OWN + slot_flat[segment_index]).astype(jnp.int32)
        picked = jnp.take(window_rows, window_index, axis=0)
        live = jnp.arange(LOC, dtype=jnp.int32) < count_flat[segment_index]
        weight = jnp.where(live, jnp.take(window_prec, window_index).astype(jnp.float32) * taper_flat[segment_index], jnp.float32(0.0))
        innov_picked = jnp.take(window_innov, window_index).astype(jnp.float32)
        ensemble_transform = transform_matrix(picked, weight, innov_picked)
        grid_width = lax.dynamic_index_in_dim(prior_lines_serial, segment_index, 1, keepdims=False)
        return apply_transform(ensemble_transform, grid_width)
    analysed = lax.map(one_block, jnp.arange(segment_total, dtype=jnp.int32))
    return jnp.transpose(analysed, (1, 0, 2)).reshape(sample_total, BOUTER, BINNER, GRID_POINTS_EACH)
```

```python
import functools

import jax
import jax.numpy as jnp
from jax import lax
from jax.experimental import pallas as pl
from jax.experimental.pallas import tpu as pltpu
from jax.sharding import PartitionSpec as P

MESH = pl.DeviceIdType.MESH
F32, BF16 = jnp.float32, jnp.bfloat16

MEMBERS = 1024
OWN = 2048
RIM = 512
WINDOW = OWN + 2 * RIM
LIST = 2560
GROUP = 16
SHARE = MEMBERS // GROUP
GRID = 1920
PARTS = 5
WIDE = GRID // PARTS
RIDGE = (MEMBERS - 1) / 1.1

PEERS = (
    (0, 1), (1, 0), (0, 3), (3, 0),
    (1, 1), (3, 3), (1, 3), (3, 1),
    (0, 2), (2, 0),
    (1, 2), (2, 1), (3, 2), (2, 3),
    (2, 2),
)
NPEER = len(PEERS)

MID = 0.5
A0 = (36 - 39 * MID + 27 * MID**2 - 9 * MID**3 + MID**4) / 16
A1 = (-39 + 54 * MID - 27 * MID**2 + 4 * MID**3) / 16
A2 = (27 - 27 * MID + 6 * MID**2) / 16
A3 = (-9 + 4 * MID) / 16
A4 = 1 / 16


def dot(left, right):
    return jnp.dot(left, right, preferred_element_type=F32)


def split(value):
    high = value.astype(BF16)
    return high, (value - high.astype(F32)).astype(BF16)


def total(value):
    return jnp.sum(value, axis=(0, 1), keepdims=True)


def eye_tile(row, col, rows, cols):
    return (row + lax.broadcasted_iota(jnp.int32, (rows, cols), 0)) == (
        col + lax.broadcasted_iota(jnp.int32, (rows, cols), 1)
    )


def row_times(mat, row, out):
    def body(c, norm):
        rows = pl.ds(pl.multiple_of(c * 128, 128), 128)
        acc = mat[rows, 0:128] * row[:, 0:128]
        for j in range(1, 8):
            acc += mat[rows, 128 * j : 128 * j + 128] * row[:, 128 * j : 128 * j + 128]
        col = jnp.sum(acc, axis=1, keepdims=True)
        out[rows, :] = jnp.broadcast_to(col, (128, 128))
        return norm + jnp.sum(col * col, axis=0, keepdims=True)

    return lax.fori_loop(0, 8, body, jnp.zeros((1, 1), F32))


def col_times(mat, col):
    def body(c, acc):
        rows = pl.ds(pl.multiple_of(c * 128, 128), 128)
        x = col[rows, :]
        return tuple(
            acc[j] + jnp.sum((mat[rows, 128 * j : 128 * j + 128] * x).reshape(16, 8, 128), axis=0)
            for j in range(8)
        )

    acc = lax.fori_loop(0, 8, body, tuple(jnp.zeros((8, 128), F32) for _ in range(8)))
    return jnp.concatenate([jnp.sum(t, axis=0, keepdims=True) for t in acc], axis=1)


def kernel(
    prior, obs, dep, prec, code, position, tally, local,
    out,
    stage, send, recv, window, turned, scaled, gram, root, trans, dev,
    temp, listed, weight, innov, column, force, rim_out, rim_in, center,
    load_sem, own_sem, obs_sem, rim_ss, rim_rs, vec_ss, vec_rs, fs, fr, bs, br, back_sem,
):
    a, b = lax.axis_index("mem"), lax.axis_index("reg")
    y, x = a // 4, a % 4

    def peer(k, sign=1):
        dy, dx = PEERS[k]
        return (((y + 4 + sign * dy) % 4) * 4 + (x + 4 + sign * dx) % 4, b)

    after = ((a + (b + 1) // 8) % GROUP, (b + 1) % 8)
    before = ((a + 15 + (b + 7) // 8) % GROUP, (b + 7) % 8)

    def lanes(c):
        return pl.ds(pl.multiple_of(c * WIDE, 128), WIDE)

    def load(c):
        slot = lax.rem(c, 2)
        return pltpu.make_async_copy(prior.at[:, :, lanes(c)], stage.at[slot], load_sem.at[slot])

    def member_rows(d):
        return pl.ds(pl.multiple_of(d * SHARE, SHARE), SHARE)

    def forward(c, k):
        to = peer(k)
        return pltpu.make_async_remote_copy(
            src_ref=send.at[c, member_rows(to[0]), :],
            dst_ref=recv.at[c, member_rows(a), :],
            send_sem=fs.at[c, k], recv_sem=fr.at[c, k],
            device_id=to, device_id_type=MESH,
        )

    def forward_own(c):
        return pltpu.make_async_copy(
            send.at[c, member_rows(a), :], recv.at[c, member_rows(a), :], own_sem.at[c]
        )

    def backward(c, k):
        to = peer(k)
        return pltpu.make_async_remote_copy(
            src_ref=send.at[c, member_rows(to[0]), :],
            dst_ref=out.at[a, :, lanes(c)],
            send_sem=bs.at[c, k], recv_sem=br.at[c, k],
            device_id=to, device_id_type=MESH,
        )

    def backward_own(c):
        return pltpu.make_async_copy(
            send.at[c, member_rows(a), :], out.at[a, :, lanes(c)], back_sem.at[c]
        )

    load(0).start()
    load(1).start()
    own_rows = pltpu.make_async_copy(obs, window.at[pl.ds(0, OWN), :], obs_sem)
    own_rows.start()

    barrier = pltpu.get_barrier_semaphore()
    for k in range(NPEER):
        pl.semaphore_signal(barrier, inc=1, device_id=peer(k), device_id_type=MESH)
    for d in (after, before):
        pl.semaphore_signal(barrier, inc=1, device_id=d, device_id_type=MESH)

    for side, first in ((0, 0), (1, 12)):
        rim_out[side, 0:4, :] = prec[first : first + 4, :]
        rim_out[side, 4:8, :] = dep[first : first + 4, :]
    weight[...] = jnp.zeros_like(weight)
    force[...] = jnp.zeros_like(force)
    innov[0:16, :] = dep[...]

    pl.semaphore_wait(barrier, NPEER + 2)

    rims = []
    for side, first, to in ((0, 0, before), (1, OWN - RIM, after)):
        where = OWN + RIM * (1 - side)
        rims.append((
            pltpu.make_async_remote_copy(
                src_ref=rim_out.at[side], dst_ref=rim_in.at[1 - side],
                send_sem=vec_ss.at[side], recv_sem=vec_rs.at[side],
                device_id=to, device_id_type=MESH,
            ),
            pltpu.make_async_remote_copy(
                src_ref=obs.at[pl.ds(first, RIM), :], dst_ref=window.at[pl.ds(where, RIM), :],
                send_sem=rim_ss.at[side], recv_sem=rim_rs.at[side],
                device_id=to, device_id_type=MESH,
            ),
        ))
    for small, large in rims:
        small.start()
        large.start()

    def send_part(c, _):
        load(c).wait()
        slot = lax.rem(c, 2)

        def shuffle(g, _):
            rows = pl.ds(pl.multiple_of(g * 16, 16), 16)
            for j in range(WIDE // 128):
                cols = slice(128 * j, 128 * j + 128)
                temp[j] = stage[slot, rows, :, cols].astype(F32).reshape(256, 128)
            for j in range(WIDE // 128):
                cols = slice(128 * j, 128 * j + 128)
                for i in range(16):
                    to_rows = pl.ds(pl.multiple_of(i * SHARE + g * 16, 16), 16)
                    send[c, to_rows, cols] = temp[j, pl.ds(i, 16, stride=16), :].astype(BF16)
            return _

        lax.fori_loop(0, SHARE // 16, shuffle, 0)
        for k in range(NPEER):
            forward(c, k).start()
        forward_own(c).start()

        @pl.when(c < PARTS - 2)
        def next_load():
            load(c + 2).start()

        return _

    lax.fori_loop(0, PARTS, send_part, 0)

    listed[...] = jnp.zeros_like(listed)
    live = tally[0, 0]

    def place(e, _):
        cols = pl.ds(pl.multiple_of(e * 512, 512), 512)
        entry = e * 512 + lax.broadcasted_iota(jnp.int32, (1, 512), 1)
        which, pos = code[:, cols], position[:, cols]
        row = jnp.where(which == 1, pos, jnp.where(which == 0, pos + RIM, pos + OWN + RIM))
        high, low = row // 128, row % 128
        value = jnp.where(entry < live, local[:, cols], 0.0)
        one = value.astype(BF16).astype(F32)
        two = (value - one).astype(BF16).astype(F32)
        three = value - one - two
        hot_low = (lax.broadcasted_iota(jnp.int32, (128, 512), 0) == low).astype(F32).astype(BF16)
        hot_high = lax.broadcasted_iota(jnp.int32, (32, 512), 0) == high
        for term in (three, two, one):
            part = jnp.where(hot_high, term, 0.0).astype(BF16)
            listed[...] += lax.dot_general(
                part, hot_low, (((1,), (1,)), ((), ())), preferred_element_type=F32
            )
        return _

    lax.fori_loop(0, LIST // 512, place, 0)

    def rows_ready(first, last):
        force_rows = (weight[first:last, :] * innov[first:last, :]).astype(BF16).astype(F32)
        for h in range(first, last):
            force[0:1, 128 * h : 128 * h + 128] = force_rows[h - first : h - first + 1, :]

        def block(h, _):
            rows = pl.ds(pl.multiple_of(h * 128, 128), 128)
            w = jnp.broadcast_to(weight[pl.ds(h, 1), :], (128, 128)).T
            for j in range(8):
                cols = slice(128 * j, 128 * j + 128)
                tile = window[rows, cols]
                scaled[rows, cols] = (tile.astype(F32) * w).astype(BF16)
                turned[cols, rows] = tile.T
            return _

        lax.fori_loop(first, last, block, 0)

    def tiles(body):
        def step(t, _):
            m = pl.multiple_of((t // 2) * 256, 256)
            n = pl.multiple_of((t % 2) * 512, 512)
            body(m, n, pl.ds(m, 256), pl.ds(n, 512))
            return _

        lax.fori_loop(0, 8, step, 0)

    weight[0:16, :] = prec[...] * listed[0:16, :]
    own_rows.wait()
    rows_ready(0, 16)

    def gram_own(m, n, rows, cols):
        gram[rows, cols] = dot(turned[rows, 0:OWN], scaled[0:OWN, cols])

    tiles(gram_own)

    for small, large in rims:
        small.wait()
        large.wait()
    for side in range(2):
        at = slice(16 + 4 * side, 20 + 4 * side)
        weight[at, :] = rim_in[side, 0:4, :] * listed[at, :]
        innov[at, :] = rim_in[side, 4:8, :]
    rows_ready(16, 24)

    def gram_rim(m, n, rows, cols):
        ridge = jnp.where(eye_tile(m, n, 256, 512), F32(RIDGE), 0.0)
        gram[rows, cols] += dot(turned[rows, OWN:WINDOW], scaled[OWN:WINDOW, cols]) + ridge

    tiles(gram_rim)
    drive = dot(force[...].astype(BF16), window[...])[0:1, :]

    row = jnp.ones((1, MEMBERS), F32)
    for step in range(3):
        norm = row_times(gram, row, column)
        column[...] = column[...] / jnp.sqrt(norm)
        row = col_times(gram, column)
        row = row / jnp.sqrt(total(row * row))
    row_times(gram, row, column)
    turned_back = jnp.concatenate(
        [column[128 * c : 128 * c + 128, :].T[0:1, :] for c in range(8)], axis=1
    )
    bound = total(row * turned_back)

    v_high, v_low, s_high = (turned.at[:, 1024 * k : 1024 * k + 1024] for k in range(3))
    s_low, q_high, q_low = (scaled.at[1024 * k : 1024 * k + 1024, :] for k in range(3))
    inverse = 1.0 / bound

    def shift(m, n, rows, cols):
        v = gram[rows, cols] * inverse - jnp.where(eye_tile(m, n, 256, 512), F32(MID), 0.0)
        gram[rows, cols] = v
        v_high[rows, cols], v_low[rows, cols] = split(v)

    tiles(shift)

    def square(m, n, rows, cols):
        s = dot(v_high[rows, :], v_low[:, cols]) + dot(v_low[rows, :], v_high[:, cols])
        s += dot(v_high[rows, :], v_high[:, cols])
        v = gram[rows, cols]
        s_high[rows, cols], s_low[rows, cols] = split(s)
        q_high[rows, cols], q_low[rows, cols] = split(A3 * v + A4 * s)
        root[rows, cols] = (
            jnp.where(eye_tile(m, n, 256, 512), F32(A0), 0.0) + A1 * v + A2 * s
        )

    tiles(square)

    def quartic(m, n, rows, cols):
        r = dot(s_high[rows, :], q_low[:, cols]) + dot(s_low[rows, :], q_high[:, cols])
        root[rows, cols] += r + dot(s_high[rows, :], q_high[:, cols])

    tiles(quartic)

    row_times(root, drive, column)
    mean = col_times(root, column) * inverse
    size = jnp.sqrt((MEMBERS - 1) * inverse)

    def finish(m, _):
        rows = pl.ds(pl.multiple_of(m * 128, 128), 128)
        trans[rows, :] = (root[rows, :] * size + mean).astype(BF16)
        return _

    lax.fori_loop(0, 8, finish, 0)

    def apply_part(c, _):
        for k in range(NPEER):
            forward(c, k).wait()
        forward_own(c).wait()

        def add(g, acc):
            rows = pl.ds(pl.multiple_of(g * 128, 128), 128)
            return acc + jnp.sum(recv[c, rows, :].astype(F32).reshape(16, 8, WIDE), axis=0)

        acc = lax.fori_loop(0, 8, add, jnp.zeros((8, WIDE), F32))
        center[...] = jnp.sum(acc, axis=0, keepdims=True) / MEMBERS

        def deviate(g, _):
            rows = pl.ds(pl.multiple_of(g * 128, 128), 128)
            dev[rows, :] = (recv[c, rows, :].astype(F32) - center[...]).astype(BF16)
            return _

        lax.fori_loop(0, 8, deviate, 0)

        def multiply(g, _):
            rows = pl.ds(pl.multiple_of(g * 256, 256), 256)
            send[c, rows, :] = (center[...] + dot(trans[rows, :], dev[...])).astype(BF16)
            return _

        lax.fori_loop(0, 4, multiply, 0)
        for k in range(NPEER):
            backward(c, k).start()
        backward_own(c).start()
        return _

    lax.fori_loop(0, PARTS, apply_part, 0)

    def drain(c, _):
        for k in range(NPEER):
            backward(c, k).wait()
        backward_own(c).wait()
        return _

    lax.fori_loop(0, PARTS, drain, 0)


def local(
    prior_samples,
    measured_anomalies,
    measured_departure,
    measure_inverse_variance,
    measure_neighbour_code,
    measure_position,
    measure_tally,
    locality_weights,
):
    hbm = pl.BlockSpec(memory_space=pl.ANY)
    vmem = pl.BlockSpec(memory_space=pltpu.VMEM)
    smem = pl.BlockSpec(memory_space=pltpu.SMEM)
    dma = pltpu.SemaphoreType.DMA
    moved = pl.pallas_call(
        kernel,
        out_shape=jax.ShapeDtypeStruct((GROUP, SHARE, GRID), BF16),
        in_specs=[hbm, hbm, vmem, vmem, vmem, vmem, smem, vmem],
        out_specs=hbm,
        scratch_shapes=[
            pltpu.VMEM((2, SHARE, GROUP, WIDE), BF16),
            pltpu.VMEM((PARTS, MEMBERS, WIDE), BF16),
            pltpu.VMEM((PARTS, MEMBERS, WIDE), BF16),
            pltpu.VMEM((WINDOW, MEMBERS), BF16),
            pltpu.VMEM((MEMBERS, WINDOW), BF16),
            pltpu.VMEM((WINDOW, MEMBERS), BF16),
            pltpu.VMEM((MEMBERS, MEMBERS), F32),
            pltpu.VMEM((MEMBERS, MEMBERS), F32),
            pltpu.VMEM((MEMBERS, MEMBERS), BF16),
            pltpu.VMEM((MEMBERS, WIDE), BF16),
            pltpu.VMEM((WIDE // 128, 256, 128), F32),
            pltpu.VMEM((32, 128), F32),
            pltpu.VMEM((24, 128), F32),
            pltpu.VMEM((24, 128), F32),
            pltpu.VMEM((MEMBERS, 128), F32),
            pltpu.VMEM((16, WINDOW), F32),
            pltpu.VMEM((2, 8, 128), F32),
            pltpu.VMEM((2, 8, 128), F32),
            pltpu.VMEM((1, WIDE), F32),
            dma((2,)), dma((PARTS,)), dma,
            dma((2,)), dma((2,)), dma((2,)), dma((2,)),
            dma((PARTS, NPEER)), dma((PARTS, NPEER)), dma((PARTS, NPEER)), dma((PARTS, NPEER)),
            dma((PARTS,)),
        ],
        compiler_params=pltpu.CompilerParams(
            collective_id=0, has_side_effects=True, vmem_limit_bytes=58 * 2**20
        ),
        cost_estimate=pl.CostEstimate(flops=24 * 10**9, bytes_accessed=12 * 2**20, transcendentals=0),
    )(
        prior_samples[:, :, 0, :],
        measured_anomalies[0, 0],
        measured_departure[0, 0].astype(F32).reshape(16, 128),
        measure_inverse_variance[0, 0].astype(F32).reshape(16, 128),
        measure_neighbour_code[0],
        measure_position[0],
        measure_tally,
        locality_weights[0],
    )
    return moved.transpose(1, 0, 2)[:, :, None, :]


def solution(mesh):
    return jax.shard_map(
        local,
        mesh=mesh,
        in_specs=(
            P("mem", None, "reg", None),
            P("mem", "reg", None, None),
            P("mem", "reg", None),
            P("mem", "reg", None),
            P("mem", "reg", None),
            P("mem", "reg", None),
            P("mem", "reg"),
            P("mem", "reg", None),
        ),
        out_specs=P("mem", None, "reg", None),
        check_vma=False,
    )
```

```python
import functools

import jax
import jax.numpy as jnp
from jax import lax
from jax.experimental import pallas as pl
from jax.experimental.pallas import tpu as pltpu
from jax.sharding import PartitionSpec as P

MESH = pl.DeviceIdType.MESH
F32, BF16 = jnp.float32, jnp.bfloat16

MEMBERS = 1024
OWN = 2048
RIM = 512
WINDOW = OWN + 2 * RIM
LIST = 2560
GROUP = 16
SHARE = MEMBERS // GROUP
GRID = 1920
PARTS = 5
WIDE = GRID // PARTS
RIDGE = (MEMBERS - 1) / 1.1

PEERS = (
    (0, 1), (1, 0), (0, 3), (3, 0),
    (1, 1), (3, 3), (1, 3), (3, 1),
    (0, 2), (2, 0),
    (1, 2), (2, 1), (3, 2), (2, 3),
    (2, 2),
)
NPEER = len(PEERS)

MID = 0.5
A0 = (36 - 39 * MID + 27 * MID**2 - 9 * MID**3 + MID**4) / 16
A1 = (-39 + 54 * MID - 27 * MID**2 + 4 * MID**3) / 16
A2 = (27 - 27 * MID + 6 * MID**2) / 16
A3 = (-9 + 4 * MID) / 16
A4 = 1 / 16


def dot(left, right):
    return jnp.dot(left, right, preferred_element_type=F32)


def split(value):
    high = value.astype(BF16)
    return high, (value - high.astype(F32)).astype(BF16)


def transpose_perm():
    to = lax.broadcasted_iota(jnp.int32, (256, 256), 0)
    source = lax.broadcasted_iota(jnp.int32, (256, 256), 1)
    return jnp.where((to % 16) * 16 + to // 16 == source, 1.0, 0.0).astype(BF16)


def total(value):
    return jnp.sum(value, axis=(0, 1), keepdims=True)


def eye_tile(row, col, rows, cols):
    return (row + lax.broadcasted_iota(jnp.int32, (rows, cols), 0)) == (
        col + lax.broadcasted_iota(jnp.int32, (rows, cols), 1)
    )


def row_times(mat, row, out):
    def body(c, norm):
        rows = pl.ds(pl.multiple_of(c * 128, 128), 128)
        acc = mat[rows, 0:128] * row[:, 0:128]
        for j in range(1, 8):
            acc += mat[rows, 128 * j : 128 * j + 128] * row[:, 128 * j : 128 * j + 128]
        col = jnp.sum(acc, axis=1, keepdims=True)
        out[rows, :] = jnp.broadcast_to(col, (128, 128))
        return norm + jnp.sum(col * col, axis=0, keepdims=True)

    return lax.fori_loop(0, 8, body, jnp.zeros((1, 1), F32))


def to_column(row, out):
    for c in range(8):
        cols = slice(128 * c, 128 * c + 128)
        out[cols, :] = jnp.broadcast_to(row[:, cols], (128, 128)).T


def col_times(mat, col):
    def body(c, acc):
        rows = pl.ds(pl.multiple_of(c * 128, 128), 128)
        x = col[rows, :]
        return tuple(
            acc[j] + jnp.sum((mat[rows, 128 * j : 128 * j + 128] * x).reshape(16, 8, 128), axis=0)
            for j in range(8)
        )

    acc = lax.fori_loop(0, 8, body, tuple(jnp.zeros((8, 128), F32) for _ in range(8)))
    return jnp.concatenate([jnp.sum(t, axis=0, keepdims=True) for t in acc], axis=1)


def kernel(
    prior, obs, dep, prec, code, position, tally, local,
    out,
    stage, send, recv, window, turned, scaled, gram, root, trans, dev, hop, hop_two,
    listed, weight, innov, column, force, rim_out, rim_in, center,
    load_sem, own_sem, obs_sem, hop_sem, rim_ss, rim_rs, vec_ss, vec_rs,
    one_ss, one_rs, two_ss, two_rs, three_ss, three_rs, fs, fr, bs, br, back_sem,
):
    a, b = lax.axis_index("mem"), lax.axis_index("reg")
    y, x = a // 4, a % 4
    plane, odd = b // 2, b % 2
    first_reg, last_reg = b == 0, b == 7

    def peer(k):
        dy, dx = PEERS[k]
        return (((y + dy) % 4) * 4 + (x + dx) % 4, b)

    after = ((a + (b + 1) // 8) % GROUP, (b + 1) % 8)
    before = ((a + 15 + (b + 7) // 8) % GROUP, (b + 7) % 8)
    partner = ((a + 15 + 2 * odd) % GROUP, b + 1 - 2 * odd)

    def remote(src, dst, send_sem, recv_sem, to):
        return pltpu.make_async_remote_copy(
            src_ref=src, dst_ref=dst, send_sem=send_sem, recv_sem=recv_sem,
            device_id=to, device_id_type=MESH,
        )

    def lanes(c):
        return pl.ds(pl.multiple_of(c * WIDE, 128), WIDE)

    def load(c):
        return pltpu.make_async_copy(prior.at[:, :, lanes(c)], stage.at[c], load_sem.at[c])

    def member_rows(d):
        return pl.ds(pl.multiple_of(d * SHARE, SHARE), SHARE)

    def forward(c, k):
        to = peer(k)
        return remote(
            send.at[c, member_rows(to[0]), :], recv.at[c, member_rows(a), :],
            fs.at[c, k], fr.at[c, k], to,
        )

    def forward_own(c):
        return pltpu.make_async_copy(
            send.at[c, member_rows(a), :], recv.at[c, member_rows(a), :], own_sem.at[c]
        )

    def backward(c, k):
        to = peer(k)
        return remote(
            send.at[c, member_rows(to[0]), :], out.at[a, :, lanes(c)], bs.at[c, k], br.at[c, k], to
        )

    def backward_own(c):
        return pltpu.make_async_copy(
            send.at[c, member_rows(a), :], out.at[a, :, lanes(c)], back_sem.at[c]
        )

    barrier = pltpu.get_barrier_semaphore()

    def greet(to):
        pl.semaphore_signal(barrier, inc=1, device_id=to, device_id_type=MESH)

    for k in range(NPEER):
        greet(peer(k))
    for k in range(1, 8):
        greet((a, (b + k) % 8))
    greet(partner)
    pl.when(first_reg)(lambda: greet(before))
    pl.when(last_reg)(lambda: greet(after))

    for c in range(PARTS):
        load(c).start()
    own_rows = pltpu.make_async_copy(obs, window.at[pl.ds(0, OWN), :], obs_sem)
    own_rows.start()
    own_piece = {
        r: pltpu.make_async_copy(obs.at[pl.ds(at, 128), :], hop, hop_sem)
        for r, at in ((0, 0), (7, OWN - 128))
    }
    for r in (0, 7):
        pl.when(b == r)(own_piece[r].start)

    weight[...] = jnp.zeros_like(weight)
    force[...] = jnp.zeros_like(force)
    for h in range(16):
        weight[h : h + 1, :] = prec[:, 128 * h : 128 * h + 128].astype(F32)
        innov[h : h + 1, :] = dep[:, 128 * h : 128 * h + 128].astype(F32)
    for side, first in ((0, 0), (1, 12)):
        rim_out[side, 0:4, :] = weight[first : first + 4, :]
        rim_out[side, 4:8, :] = innov[first : first + 4, :]

    perm = transpose_perm()

    def arrange(c, _):
        load(c).wait()

        def shuffle(g, _):
            rows = pl.ds(pl.multiple_of(g * 16, 16), 16)
            moved = dot(perm, stage[c, rows, :, :].reshape(256, WIDE)).astype(BF16)
            for i in range(16):
                to_rows = pl.ds(pl.multiple_of(i * SHARE + g * 16, 16), 16)
                send[c, to_rows, :] = moved[16 * i : 16 * i + 16, :]
            return _

        return lax.fori_loop(0, SHARE // 16, shuffle, _)

    lax.fori_loop(0, PARTS, arrange, 0)

    listed[...] = jnp.zeros_like(listed)
    live = tally[0, 0]

    def place(e, _):
        cols = pl.ds(pl.multiple_of(e * 512, 512), 512)
        entry = e * 512 + lax.broadcasted_iota(jnp.int32, (1, 512), 1)
        which, pos = code[:, cols], position[:, cols]
        row = jnp.where(which == 1, pos, jnp.where(which == 0, pos + RIM, pos + OWN + RIM))
        high, low = row // 128, row % 128
        value = jnp.where(entry < live, local[:, cols], 0.0)
        one = value.astype(BF16).astype(F32)
        two = (value - one).astype(BF16).astype(F32)
        three = value - one - two
        hot_low = (lax.broadcasted_iota(jnp.int32, (128, 512), 0) == low).astype(F32).astype(BF16)
        hot_high = lax.broadcasted_iota(jnp.int32, (32, 512), 0) == high
        for term in (three, two, one):
            part = jnp.where(hot_high, term, 0.0).astype(BF16)
            listed[...] += lax.dot_general(
                part, hot_low, (((1,), (1,)), ((), ())), preferred_element_type=F32
            )
        return _

    lax.fori_loop(0, LIST // 512, place, 0)
    weight[0:16, :] = weight[0:16, :] * listed[0:16, :]

    @pl.when(b % 7 != 0)
    def wait_inner():
        pl.semaphore_wait(barrier, NPEER + 8)

    @pl.when(b % 7 == 0)
    def wait_end():
        pl.semaphore_wait(barrier, NPEER + 9)

    small = [
        remote(rim_out.at[side], rim_in.at[1 - side], vec_ss.at[side], vec_rs.at[side], to)
        for side, to in ((0, before), (1, after))
    ]
    large = [
        remote(
            obs.at[pl.ds(at, RIM), :], window.at[pl.ds(OWN + RIM * (1 - side), RIM), :],
            rim_ss.at[side], rim_rs.at[side], (a, to),
        )
        for side, at, to in ((0, 0, (b + 7) % 8), (1, OWN - RIM, (b + 1) % 8))
    ]
    step_one = {
        r: [
            remote(obs.at[pl.ds(at + 128 * q, 128), :], hop, one_ss.at[n], one_rs, (a, 2 * q + r // 7))
            for n, q in enumerate(pieces)
        ]
        for r, at, pieces in ((0, 0, (1, 2, 3)), (7, OWN - RIM, (0, 1, 2)))
    }
    step_two = remote(hop, hop_two, two_ss, two_rs, partner)
    piece_rows = pl.ds(pl.multiple_of(OWN + RIM * odd + 128 * plane, 128), 128)
    step_three = remote(
        hop_two, window.at[piece_rows, :], three_ss, three_rs.at[plane], (a, 7 * odd)
    )
    last_step = {
        r: [
            remote(
                hop_two, window.at[pl.ds(at + 128 * q, 128), :], three_ss, three_rs.at[q], (a, r)
            )
            for q in pieces
        ]
        for r, at, pieces in ((0, OWN, (1, 2, 3)), (7, OWN + RIM, (0, 1, 2)))
    }

    for r in (0, 7):
        pl.when(b == r)(lambda r=r: [copy.start() for copy in step_one[r]] and None)
    for copy in small:
        copy.start()
    pl.when(b > 0)(large[0].start)
    pl.when(b < 7)(large[1].start)

    def send_part(c, _):
        for k in range(NPEER):
            forward(c, k).start()
        forward_own(c).start()
        return _

    send_part(0, 0)

    def rows_ready(first, last):
        force_rows = (weight[first:last, :] * innov[first:last, :]).astype(BF16).astype(F32)
        for h in range(first, last):
            force[0:1, 128 * h : 128 * h + 128] = force_rows[h - first : h - first + 1, :]

        def block(h, _):
            rows = pl.ds(pl.multiple_of(h * 128, 128), 128)
            w = jnp.broadcast_to(weight[pl.ds(h, 1), :], (128, 128)).T
            for j in range(8):
                cols = slice(128 * j, 128 * j + 128)
                tile = window[rows, cols]
                scaled[rows, cols] = (tile.astype(F32) * w).astype(BF16)
                turned[cols, rows] = tile.T
            return _

        lax.fori_loop(first, last, block, 0)

    def halves(body):
        def step(t, _):
            n = pl.multiple_of(t * 512, 512)
            body(n, pl.ds(n, 512))
            return _

        lax.fori_loop(0, 2, step, 0)

    def tiles(body):
        def step(t, _):
            m = pl.multiple_of(t * 128, 128)
            body(m, pl.ds(m, 128))
            return _

        lax.fori_loop(0, 8, step, 0)

    own_rows.wait()
    rows_ready(0, 16)
    gram[:, 0:512] = dot(turned[:, 0:OWN], scaled[0:OWN, 0:512])

    for r in (0, 7):
        pl.when(b == r)(own_piece[r].wait)
    pl.when(b % 7 != 0)(step_one[7][0].wait_recv)
    step_two.start()
    lax.fori_loop(1, PARTS, send_part, 0)

    gram[:, 512:1024] = dot(turned[:, 0:OWN], scaled[0:OWN, 512:1024])

    step_two.wait()

    @pl.when(b % 7 != 0)
    def pass_on():
        step_three.start()

    @pl.when(b % 7 == 0)
    def keep():
        window[piece_rows, :] = hop_two[...]

    for copy in small:
        copy.wait()
    pl.when(b < 7)(large[0].wait_recv)
    pl.when(b > 0)(large[1].wait_recv)
    for r in (0, 7):
        pl.when(b == r)(lambda r=r: [copy.wait_recv() for copy in last_step[r]] and None)
    for side in range(2):
        at = slice(16 + 4 * side, 20 + 4 * side)
        weight[at, :] = rim_in[side, 0:4, :] * listed[at, :]
        innov[at, :] = rim_in[side, 4:8, :]
    rows_ready(16, 24)

    high, low, s_high = (turned.at[:, 1024 * k : 1024 * k + 1024] for k in range(3))
    s_low, q_high, q_low = (scaled.at[1024 * k : 1024 * k + 1024, :] for k in range(3))

    def gram_rim(n, cols):
        ridge = jnp.where(eye_tile(0, n, 1024, 512), F32(RIDGE), 0.0)
        system = gram[:, cols] + dot(turned[:, OWN:WINDOW], scaled[OWN:WINDOW, cols]) + ridge
        gram[:, cols] = system
        high[:, cols], low[:, cols] = split(system)

    halves(gram_rim)
    drive = dot(force[...].astype(BF16), window[...])[0:1, :]

    def square(n, cols):
        root[:, cols] = dot(high[...], low[:, cols]) + dot(low[...], high[:, cols])
        root[:, cols] += dot(high[...], high[:, cols])

    halves(square)

    norm = row_times(root, jnp.ones((1, MEMBERS), F32), column)
    column[...] = column[...] / jnp.sqrt(norm)
    row = col_times(root, column)
    row = row / jnp.sqrt(total(row * row))
    norm = row_times(root, row, column)
    column[...] = column[...] / jnp.sqrt(norm)
    probe = jnp.concatenate(
        [column[128 * c : 128 * c + 128, :].T[0:1, :] for c in range(8)], axis=1
    )
    bound = total(probe * col_times(gram, column))
    inverse = 1.0 / bound

    def factors(m, rows):
        diagonal = eye_tile(m, 0, 128, 1024)
        unit = gram[rows, :] * inverse
        v = unit - jnp.where(diagonal, F32(MID), 0.0)
        s = root[rows, :] * (inverse * inverse) - 2 * MID * unit
        s += jnp.where(diagonal, F32(MID * MID), 0.0)
        s_high[rows, :], s_low[rows, :] = split(s)
        q_high[rows, :], q_low[rows, :] = split(A3 * v + A4 * s)
        root[rows, :] = jnp.where(diagonal, F32(A0), 0.0) + A1 * v + A2 * s

    tiles(factors)

    def quartic(n, cols):
        root[:, cols] += dot(s_high[...], q_low[:, cols]) + dot(s_low[...], q_high[:, cols])
        root[:, cols] += dot(s_high[...], q_high[:, cols])

    halves(quartic)

    to_column(drive, column)
    to_column(col_times(root, column), column)
    mean = col_times(root, column) * inverse
    size = jnp.sqrt((MEMBERS - 1) * inverse)

    def finish(m, rows):
        trans[rows, :] = (root[rows, :] * size + mean).astype(BF16)

    tiles(finish)

    def apply_part(c, _):
        for k in range(NPEER):
            forward(c, k).wait()
        forward_own(c).wait()

        def add(g, acc):
            rows = pl.ds(pl.multiple_of(g * 128, 128), 128)
            return acc + jnp.sum(recv[c, rows, :].astype(F32).reshape(16, 8, WIDE), axis=0)

        acc = lax.fori_loop(0, 8, add, jnp.zeros((8, WIDE), F32))
        center[...] = jnp.sum(acc, axis=0, keepdims=True) / MEMBERS

        def deviate(g, _):
            rows = pl.ds(pl.multiple_of(g * 128, 128), 128)
            dev[rows, :] = (recv[c, rows, :].astype(F32) - center[...]).astype(BF16)
            return _

        lax.fori_loop(0, 8, deviate, 0)
        send[c] = (center[...] + dot(trans[...], dev[...])).astype(BF16)
        for k in range(NPEER):
            backward(c, k).start()
        backward_own(c).start()
        return _

    lax.fori_loop(0, PARTS, apply_part, 0)

    pl.when(b > 0)(large[0].wait_send)
    pl.when(b < 7)(large[1].wait_send)
    for r in (0, 7):
        pl.when(b == r)(lambda r=r: [copy.wait_send() for copy in step_one[r]] and None)
    pl.when(b % 7 != 0)(step_three.wait_send)

    def drain(c, _):
        for k in range(NPEER):
            backward(c, k).wait()
        backward_own(c).wait()
        return _

    lax.fori_loop(0, PARTS, drain, 0)


def finish_kernel(moved, out, buffer, sem):
    def store(g):
        return pltpu.make_async_copy(buffer.at[g], out.at[pl.ds(16 * g, 16)], sem.at[g])

    perm = transpose_perm()
    for g in range(SHARE // 16):
        rows = moved[:, 16 * g : 16 * g + 16, :].reshape(256, GRID)
        buffer[g] = dot(perm, rows).astype(BF16).reshape(16, 16, GRID)
        store(g).start()
    for g in range(SHARE // 16):
        store(g).wait()


def local(
    prior_samples,
    measured_anomalies,
    measured_departure,
    measure_inverse_variance,
    measure_neighbour_code,
    measure_position,
    measure_tally,
    locality_weights,
):
    hbm = pl.BlockSpec(memory_space=pl.ANY)
    vmem = pl.BlockSpec(memory_space=pltpu.VMEM)
    smem = pl.BlockSpec(memory_space=pltpu.SMEM)
    dma = pltpu.SemaphoreType.DMA
    moved = pl.pallas_call(
        kernel,
        out_shape=pltpu.VMEM((GROUP, SHARE, GRID), BF16),
        in_specs=[hbm, hbm, vmem, vmem, vmem, vmem, smem, vmem],
        out_specs=vmem,
        scratch_shapes=[
            pltpu.VMEM((PARTS, SHARE, GROUP, WIDE), BF16),
            pltpu.VMEM((PARTS, MEMBERS, WIDE), BF16),
            pltpu.VMEM((PARTS, MEMBERS, WIDE), BF16),
            pltpu.VMEM((WINDOW, MEMBERS), BF16),
            pltpu.VMEM((MEMBERS, WINDOW), BF16),
            pltpu.VMEM((WINDOW, MEMBERS), BF16),
            pltpu.VMEM((MEMBERS, MEMBERS), F32),
            pltpu.VMEM((MEMBERS, MEMBERS), F32),
            pltpu.VMEM((MEMBERS, MEMBERS), BF16),
            pltpu.VMEM((MEMBERS, WIDE), BF16),
            pltpu.VMEM((128, MEMBERS), BF16),
            pltpu.VMEM((128, MEMBERS), BF16),
            pltpu.VMEM((32, 128), F32),
            pltpu.VMEM((24, 128), F32),
            pltpu.VMEM((24, 128), F32),
            pltpu.VMEM((MEMBERS, 128), F32),
            pltpu.VMEM((16, WINDOW), F32),
            pltpu.VMEM((2, 8, 128), F32),
            pltpu.VMEM((2, 8, 128), F32),
            pltpu.VMEM((1, WIDE), F32),
            dma((PARTS,)), dma((PARTS,)), dma, dma,
            dma((2,)), dma((2,)), dma((2,)), dma((2,)),
            dma((3,)), dma, dma, dma, dma, dma((4,)),
            dma((PARTS, NPEER)), dma((PARTS, NPEER)), dma((PARTS, NPEER)), dma((PARTS, NPEER)),
            dma((PARTS,)),
        ],
        compiler_params=pltpu.CompilerParams(
            collective_id=0, has_side_effects=True, vmem_limit_bytes=54 * 2**20
        ),
        cost_estimate=pl.CostEstimate(flops=24 * 10**9, bytes_accessed=12 * 2**20, transcendentals=0),
    )(
        prior_samples[:, :, 0, :],
        measured_anomalies[0, 0],
        measured_departure[0],
        measure_inverse_variance[0],
        measure_neighbour_code[0],
        measure_position[0],
        measure_tally,
        locality_weights[0],
    )
    out = pl.pallas_call(
        finish_kernel,
        out_shape=jax.ShapeDtypeStruct((SHARE, GROUP, GRID), BF16),
        in_specs=[vmem],
        out_specs=hbm,
        scratch_shapes=[pltpu.VMEM((SHARE // 16, 16, GROUP, GRID), BF16), dma((SHARE // 16,))],
        compiler_params=pltpu.CompilerParams(vmem_limit_bytes=20 * 2**20),
        cost_estimate=pl.CostEstimate(flops=10**9, bytes_accessed=8 * 2**20, transcendentals=0),
    )(moved)
    return out[:, :, None, :]


def solution(mesh):
    return jax.shard_map(
        local,
        mesh=mesh,
        in_specs=(
            P("mem", None, "reg", None),
            P("mem", "reg", None, None),
            P("mem", "reg", None),
            P("mem", "reg", None),
            P("mem", "reg", None),
            P("mem", "reg", None),
            P("mem", "reg"),
            P("mem", "reg", None),
        ),
        out_specs=P("mem", None, "reg", None),
        check_vma=False,
    )
```

```python
import functools

import jax
import jax.numpy as jnp
from jax import lax
from jax.experimental import pallas as pl
from jax.experimental.pallas import tpu as pltpu
from jax.sharding import PartitionSpec as P

MESH = pl.DeviceIdType.MESH
F32, BF16 = jnp.float32, jnp.bfloat16

MEMBERS = 1024
OWN = 2048
RIM = 512
WINDOW = OWN + 2 * RIM
LIST = 2560
GROUP = 16
SHARE = MEMBERS // GROUP
GRID = 1920
PARTS = 5
WIDE = GRID // PARTS
RIDGE = (MEMBERS - 1) / 1.1

PEERS = (
    (0, 1), (1, 0), (0, 3), (3, 0),
    (1, 1), (3, 3), (1, 3), (3, 1),
    (0, 2), (2, 0),
    (1, 2), (2, 1), (3, 2), (2, 3),
    (2, 2),
)
NPEER = len(PEERS)
FEW = 15

MID = 0.5
A0 = (36 - 39 * MID + 27 * MID**2 - 9 * MID**3 + MID**4) / 16
A1 = (-39 + 54 * MID - 27 * MID**2 + 4 * MID**3) / 16
A2 = (27 - 27 * MID + 6 * MID**2) / 16
A3 = (-9 + 4 * MID) / 16
A4 = 1 / 16


def dot(left, right):
    return jnp.dot(left, right, preferred_element_type=F32)


def split(value):
    high = value.astype(BF16)
    return high, (value - high.astype(F32)).astype(BF16)


def transpose_perm():
    to = lax.broadcasted_iota(jnp.int32, (256, 256), 0)
    source = lax.broadcasted_iota(jnp.int32, (256, 256), 1)
    return jnp.where((to % 16) * 16 + to // 16 == source, 1.0, 0.0).astype(BF16)


def total(value):
    return jnp.sum(value, axis=(0, 1), keepdims=True)


def eye_tile(row, col, rows, cols):
    return (row + lax.broadcasted_iota(jnp.int32, (rows, cols), 0)) == (
        col + lax.broadcasted_iota(jnp.int32, (rows, cols), 1)
    )


def row_times(mat, row, out):
    def body(c, norm):
        rows = pl.ds(pl.multiple_of(c * 128, 128), 128)
        acc = mat[rows, 0:128] * row[:, 0:128]
        for j in range(1, 8):
            acc += mat[rows, 128 * j : 128 * j + 128] * row[:, 128 * j : 128 * j + 128]
        col = jnp.sum(acc, axis=1, keepdims=True)
        out[rows, :] = jnp.broadcast_to(col, (128, 128))
        return norm + jnp.sum(col * col, axis=0, keepdims=True)

    return lax.fori_loop(0, 8, body, jnp.zeros((1, 1), F32))


def to_column(row, out):
    for c in range(8):
        cols = slice(128 * c, 128 * c + 128)
        out[cols, :] = jnp.broadcast_to(row[:, cols], (128, 128)).T


def col_times(mat, col):
    def body(c, acc):
        rows = pl.ds(pl.multiple_of(c * 128, 128), 128)
        x = col[rows, :]
        return tuple(
            acc[j] + jnp.sum((mat[rows, 128 * j : 128 * j + 128] * x).reshape(16, 8, 128), axis=0)
            for j in range(8)
        )

    acc = lax.fori_loop(0, 8, body, tuple(jnp.zeros((8, 128), F32) for _ in range(8)))
    return jnp.concatenate([jnp.sum(t, axis=0, keepdims=True) for t in acc], axis=1)


def kernel(
    prior, obs, dep, prec, code, position, tally, local,
    out,
    stage, send, recv, window, turned, scaled, gram, root, trans, dev, hop, hop_two,
    listed, weight, innov, column, force, rim_out, rim_in, center,
    load_sem, own_sem, obs_sem, hop_sem, rim_ss, rim_rs, vec_ss, vec_rs,
    one_ss, one_rs, two_ss, two_rs, three_ss, three_rs, fs, fr, bs, br, back_sem,
):
    a, b = lax.axis_index("mem"), lax.axis_index("reg")
    y, x = a // 4, a % 4
    plane, odd = b // 2, b % 2
    first_reg, last_reg = b == 0, b == 7

    def peer(k):
        dy, dx = PEERS[k]
        return (((y + dy) % 4) * 4 + (x + dx) % 4, b)

    after = ((a + (b + 1) // 8) % GROUP, (b + 1) % 8)
    before = ((a + 15 + (b + 7) // 8) % GROUP, (b + 7) % 8)
    partner = ((a + 15 + 2 * odd) % GROUP, b + 1 - 2 * odd)

    def remote(src, dst, send_sem, recv_sem, to):
        return pltpu.make_async_remote_copy(
            src_ref=src, dst_ref=dst, send_sem=send_sem, recv_sem=recv_sem,
            device_id=to, device_id_type=MESH,
        )

    def lanes(c):
        return pl.ds(pl.multiple_of(c * WIDE, 128), WIDE)

    def load(c):
        return pltpu.make_async_copy(prior.at[:, :, lanes(c)], stage.at[c], load_sem.at[c])

    def member_rows(d):
        return pl.ds(pl.multiple_of(d * SHARE, SHARE), SHARE)

    def forward(c, k):
        to = peer(k)
        return remote(
            send.at[c, member_rows(to[0]), :], recv.at[c, member_rows(a), :],
            fs.at[c, k], fr.at[c, k], to,
        )

    def forward_own(c):
        return pltpu.make_async_copy(
            send.at[c, member_rows(a), :], recv.at[c, member_rows(a), :], own_sem.at[c]
        )

    def backward(c, k):
        to = peer(k)
        return remote(
            send.at[c, member_rows(to[0]), :], out.at[a, :, lanes(c)], bs.at[c, k], br.at[c, k], to
        )

    def backward_own(c):
        return pltpu.make_async_copy(
            send.at[c, member_rows(a), :], out.at[a, :, lanes(c)], back_sem.at[c]
        )

    barrier = pltpu.get_barrier_semaphore()

    def greet(to):
        pl.semaphore_signal(barrier, inc=1, device_id=to, device_id_type=MESH)

    for k in range(NPEER):
        greet(peer(k))
    for k in range(1, 8):
        greet((a, (b + k) % 8))
    greet(partner)
    pl.when(first_reg)(lambda: greet(before))
    pl.when(last_reg)(lambda: greet(after))

    for c in range(PARTS):
        load(c).start()
    own_rows = pltpu.make_async_copy(obs, window.at[pl.ds(0, OWN), :], obs_sem)
    own_rows.start()
    own_piece = {
        r: pltpu.make_async_copy(obs.at[pl.ds(at, 128), :], hop, hop_sem)
        for r, at in ((0, 0), (7, OWN - 128))
    }
    for r in (0, 7):
        pl.when(b == r)(own_piece[r].start)

    weight[...] = jnp.zeros_like(weight)
    force[...] = jnp.zeros_like(force)
    for h in range(16):
        weight[h : h + 1, :] = prec[:, 128 * h : 128 * h + 128].astype(F32)
        innov[h : h + 1, :] = dep[:, 128 * h : 128 * h + 128].astype(F32)
    for side, first in ((0, 0), (1, 12)):
        rim_out[side, 0:4, :] = weight[first : first + 4, :]
        rim_out[side, 4:8, :] = innov[first : first + 4, :]

    perm = transpose_perm()

    def arrange(c, _):
        load(c).wait()

        def shuffle(g, _):
            rows = pl.ds(pl.multiple_of(g * 16, 16), 16)
            moved = dot(perm, stage[c, rows, :, :].reshape(256, WIDE)).astype(BF16)
            for i in range(16):
                to_rows = pl.ds(pl.multiple_of(i * SHARE + g * 16, 16), 16)
                send[c, to_rows, :] = moved[16 * i : 16 * i + 16, :]
            return _

        return lax.fori_loop(0, SHARE // 16, shuffle, _)

    arrange(0, 0)

    @pl.when(b % 7 != 0)
    def wait_inner():
        pl.semaphore_wait(barrier, NPEER + 8)

    @pl.when(b % 7 == 0)
    def wait_end():
        pl.semaphore_wait(barrier, NPEER + 9)

    small = [
        remote(rim_out.at[side], rim_in.at[1 - side], vec_ss.at[side], vec_rs.at[side], to)
        for side, to in ((0, before), (1, after))
    ]
    large = [
        remote(
            obs.at[pl.ds(at, RIM), :], window.at[pl.ds(OWN + RIM * (1 - side), RIM), :],
            rim_ss.at[side], rim_rs.at[side], (a, to),
        )
        for side, at, to in ((0, 0, (b + 7) % 8), (1, OWN - RIM, (b + 1) % 8))
    ]
    step_one = {
        r: [
            remote(obs.at[pl.ds(at + 128 * q, 128), :], hop, one_ss.at[n], one_rs, (a, 2 * q + r // 7))
            for n, q in enumerate(pieces)
        ]
        for r, at, pieces in ((0, 0, (1, 2, 3)), (7, OWN - RIM, (0, 1, 2)))
    }
    step_two = remote(hop, hop_two, two_ss, two_rs, partner)
    piece_rows = pl.ds(pl.multiple_of(OWN + RIM * odd + 128 * plane, 128), 128)
    step_three = remote(
        hop_two, window.at[piece_rows, :], three_ss, three_rs.at[plane], (a, 7 * odd)
    )
    last_step = {
        r: [
            remote(
                hop_two, window.at[pl.ds(at + 128 * q, 128), :], three_ss, three_rs.at[q], (a, r)
            )
            for q in pieces
        ]
        for r, at, pieces in ((0, OWN, (1, 2, 3)), (7, OWN + RIM, (0, 1, 2)))
    }

    for r in (0, 7):
        pl.when(b == r)(lambda r=r: [copy.start() for copy in step_one[r]] and None)
    for copy in small:
        copy.start()

    pl.when(odd == 1)(large[0].start)
    pl.when(odd == 0)(large[1].start)

    for k in range(FEW):
        forward(0, k).start()
    forward_own(0).start()
    lax.fori_loop(1, PARTS, arrange, 0)
    listed[...] = jnp.zeros_like(listed)
    live = tally[0, 0]

    def place(e, _):
        cols = pl.ds(pl.multiple_of(e * 512, 512), 512)
        entry = e * 512 + lax.broadcasted_iota(jnp.int32, (1, 512), 1)
        which, pos = code[:, cols], position[:, cols]
        row = jnp.where(which == 1, pos, jnp.where(which == 0, pos + RIM, pos + OWN + RIM))
        high, low = row // 128, row % 128
        value = jnp.where(entry < live, local[:, cols], 0.0)
        one = value.astype(BF16).astype(F32)
        two = (value - one).astype(BF16).astype(F32)
        three = value - one - two
        hot_low = (lax.broadcasted_iota(jnp.int32, (128, 512), 0) == low).astype(F32).astype(BF16)
        hot_high = lax.broadcasted_iota(jnp.int32, (32, 512), 0) == high
        for term in (three, two, one):
            part = jnp.where(hot_high, term, 0.0).astype(BF16)
            listed[...] += lax.dot_general(
                part, hot_low, (((1,), (1,)), ((), ())), preferred_element_type=F32
            )
        return _

    lax.fori_loop(0, LIST // 512, place, 0)
    weight[0:16, :] = weight[0:16, :] * listed[0:16, :]

    def send_part(c, _):
        for k in range(NPEER):
            forward(c, k).start()
        forward_own(c).start()
        return _

    for r in (0, 7):
        pl.when(b == r)(own_piece[r].wait)
    pl.when(b % 7 != 0)(step_one[7][0].wait_recv)
    step_two.start()
    pl.when((odd == 0) & (b > 0))(large[0].start)
    pl.when((odd == 1) & (b < 7))(large[1].start)
    for k in range(FEW, NPEER):
        forward(0, k).start()
    lax.fori_loop(1, PARTS, send_part, 0)

    def rows_ready(first, last):
        force_rows = (weight[first:last, :] * innov[first:last, :]).astype(BF16).astype(F32)
        for h in range(first, last):
            force[0:1, 128 * h : 128 * h + 128] = force_rows[h - first : h - first + 1, :]

        def block(h, _):
            rows = pl.ds(pl.multiple_of(h * 128, 128), 128)
            w = jnp.broadcast_to(weight[pl.ds(h, 1), :], (128, 128)).T
            for j in range(8):
                cols = slice(128 * j, 128 * j + 128)
                tile = window[rows, cols]
                scaled[rows, cols] = (tile.astype(F32) * w).astype(BF16)
                turned[cols, rows] = tile.T
            return _

        lax.fori_loop(first, last, block, 0)

    def halves(body):
        def step(t, _):
            n = pl.multiple_of(t * 512, 512)
            body(n, pl.ds(n, 512))
            return _

        lax.fori_loop(0, 2, step, 0)

    def tiles(body):
        def step(t, _):
            m = pl.multiple_of(t * 128, 128)
            body(m, pl.ds(m, 128))
            return _

        lax.fori_loop(0, 8, step, 0)

    own_rows.wait()
    rows_ready(0, 16)


    def gram_own(n, cols):
        gram[:, cols] = dot(turned[:, 0:OWN], scaled[0:OWN, cols])

    halves(gram_own)
    drive = dot(force[:, 0:OWN].astype(BF16), window[0:OWN, :])

    step_two.wait()

    @pl.when(b % 7 != 0)
    def pass_on():
        step_three.start()

    @pl.when(b % 7 == 0)
    def keep():
        window[piece_rows, :] = hop_two[...]

    for copy in small:
        copy.wait()
    pl.when(b < 7)(large[0].wait_recv)
    pl.when(b > 0)(large[1].wait_recv)
    for r in (0, 7):
        pl.when(b == r)(lambda r=r: [copy.wait_recv() for copy in last_step[r]] and None)
    for side in range(2):
        at = slice(16 + 4 * side, 20 + 4 * side)
        weight[at, :] = rim_in[side, 0:4, :] * listed[at, :]
        innov[at, :] = rim_in[side, 4:8, :]
    rows_ready(16, 24)

    high, low, square_bf = (turned.at[:, 1024 * k : 1024 * k + 1024] for k in range(3))
    cubic_bf = scaled.at[0:1024, :]

    def gram_rim(n, cols):
        ridge = jnp.where(eye_tile(0, n, 1024, 512), F32(RIDGE), 0.0)
        system = gram[:, cols] + dot(turned[:, OWN:WINDOW], scaled[OWN:WINDOW, cols]) + ridge
        gram[:, cols] = system
        high[:, cols], low[:, cols] = split(system)

    halves(gram_rim)
    drive += dot(force[:, OWN:WINDOW].astype(BF16), window[OWN:WINDOW, :])

    def square(n, cols):
        root[:, cols] = dot(high[...], low[:, cols]) + dot(low[...], high[:, cols])
        root[:, cols] += dot(high[...], high[:, cols])

    halves(square)

    norm = row_times(root, jnp.ones((1, MEMBERS), F32), column)
    column[...] = column[...] / jnp.sqrt(norm)
    row = col_times(root, column)
    row = row / jnp.sqrt(total(row * row))
    norm = row_times(root, row, column)
    column[...] = column[...] / jnp.sqrt(norm)
    probe = jnp.concatenate(
        [column[128 * c : 128 * c + 128, :].T[0:1, :] for c in range(8)], axis=1
    )
    bound = total(probe * col_times(gram, column))
    inverse = 1.0 / bound

    def factors(m, rows):
        diagonal = eye_tile(m, 0, 128, 1024)
        unit = gram[rows, :] * inverse
        v = unit - jnp.where(diagonal, F32(MID), 0.0)
        s = root[rows, :] * (inverse * inverse) - 2 * MID * unit
        s += jnp.where(diagonal, F32(MID * MID), 0.0)
        square_bf[rows, :] = s.astype(BF16)
        cubic_bf[rows, :] = (A3 * v + A4 * s).astype(BF16)
        root[rows, :] = jnp.where(diagonal, F32(A0), 0.0) + A1 * v + A2 * s

    tiles(factors)

    def quartic(n, cols):
        root[:, cols] += dot(square_bf[...], cubic_bf[:, cols])

    halves(quartic)

    to_column(drive[0:1, :], column)
    to_column(col_times(root, column), column)
    mean = col_times(root, column) * inverse
    size = jnp.sqrt((MEMBERS - 1) * inverse)

    def finish(m, rows):
        trans[rows, :] = (root[rows, :] * size + mean).astype(BF16)

    tiles(finish)

    def apply_part(c, _):
        for k in range(NPEER):
            forward(c, k).wait()
        forward_own(c).wait()

        def add(g, acc):
            rows = pl.ds(pl.multiple_of(g * 128, 128), 128)
            return acc + jnp.sum(recv[c, rows, :].astype(F32).reshape(16, 8, WIDE), axis=0)

        acc = lax.fori_loop(0, 8, add, jnp.zeros((8, WIDE), F32))
        center[...] = jnp.sum(acc, axis=0, keepdims=True) / MEMBERS

        def deviate(g, _):
            rows = pl.ds(pl.multiple_of(g * 128, 128), 128)
            dev[rows, :] = (recv[c, rows, :].astype(F32) - center[...]).astype(BF16)
            return _

        lax.fori_loop(0, 8, deviate, 0)
        send[c] = (center[...] + dot(trans[...], dev[...])).astype(BF16)
        for k in range(NPEER):
            backward(c, k).start()
        backward_own(c).start()
        return _

    lax.fori_loop(0, PARTS, apply_part, 0)

    pl.when(b > 0)(large[0].wait_send)
    pl.when(b < 7)(large[1].wait_send)
    for r in (0, 7):
        pl.when(b == r)(lambda r=r: [copy.wait_send() for copy in step_one[r]] and None)
    pl.when(b % 7 != 0)(step_three.wait_send)

    def drain(c, _):
        for k in range(NPEER):
            backward(c, k).wait()
        backward_own(c).wait()
        return _

    lax.fori_loop(0, PARTS, drain, 0)


def finish_kernel(moved, out, buffer, sem):
    def store(g):
        return pltpu.make_async_copy(buffer.at[g], out.at[pl.ds(16 * g, 16)], sem.at[g])

    perm = transpose_perm()
    for g in range(SHARE // 16):
        rows = moved[:, 16 * g : 16 * g + 16, :].reshape(256, GRID)
        buffer[g] = dot(perm, rows).astype(BF16).reshape(16, 16, GRID)
        store(g).start()
    for g in range(SHARE // 16):
        store(g).wait()


def local(
    prior_samples,
    measured_anomalies,
    measured_departure,
    measure_inverse_variance,
    measure_neighbour_code,
    measure_position,
    measure_tally,
    locality_weights,
):
    hbm = pl.BlockSpec(memory_space=pl.ANY)
    vmem = pl.BlockSpec(memory_space=pltpu.VMEM)
    smem = pl.BlockSpec(memory_space=pltpu.SMEM)
    dma = pltpu.SemaphoreType.DMA
    moved = pl.pallas_call(
        kernel,
        out_shape=pltpu.VMEM((GROUP, SHARE, GRID), BF16),
        in_specs=[hbm, hbm, vmem, vmem, vmem, vmem, smem, vmem],
        out_specs=vmem,
        scratch_shapes=[
            pltpu.VMEM((PARTS, SHARE, GROUP, WIDE), BF16),
            pltpu.VMEM((PARTS, MEMBERS, WIDE), BF16),
            pltpu.VMEM((PARTS, MEMBERS, WIDE), BF16),
            pltpu.VMEM((WINDOW, MEMBERS), BF16),
            pltpu.VMEM((MEMBERS, WINDOW), BF16),
            pltpu.VMEM((WINDOW, MEMBERS), BF16),
            pltpu.VMEM((MEMBERS, MEMBERS), F32),
            pltpu.VMEM((MEMBERS, MEMBERS), F32),
            pltpu.VMEM((MEMBERS, MEMBERS), BF16),
            pltpu.VMEM((MEMBERS, WIDE), BF16),
            pltpu.VMEM((128, MEMBERS), BF16),
            pltpu.VMEM((128, MEMBERS), BF16),
            pltpu.VMEM((32, 128), F32),
            pltpu.VMEM((24, 128), F32),
            pltpu.VMEM((24, 128), F32),
            pltpu.VMEM((MEMBERS, 128), F32),
            pltpu.VMEM((16, WINDOW), F32),
            pltpu.VMEM((2, 8, 128), F32),
            pltpu.VMEM((2, 8, 128), F32),
            pltpu.VMEM((1, WIDE), F32),
            dma((PARTS,)), dma((PARTS,)), dma, dma,
            dma((2,)), dma((2,)), dma((2,)), dma((2,)),
            dma((3,)), dma, dma, dma, dma, dma((4,)),
            dma((PARTS, NPEER)), dma((PARTS, NPEER)), dma((PARTS, NPEER)), dma((PARTS, NPEER)),
            dma((PARTS,)),
        ],
        compiler_params=pltpu.CompilerParams(
            collective_id=0, has_side_effects=True, vmem_limit_bytes=54 * 2**20
        ),
        cost_estimate=pl.CostEstimate(flops=24 * 10**9, bytes_accessed=12 * 2**20, transcendentals=0),
    )(
        prior_samples[:, :, 0, :],
        measured_anomalies[0, 0],
        measured_departure[0],
        measure_inverse_variance[0],
        measure_neighbour_code[0],
        measure_position[0],
        measure_tally,
        locality_weights[0],
    )
    out = pl.pallas_call(
        finish_kernel,
        out_shape=jax.ShapeDtypeStruct((SHARE, GROUP, GRID), BF16),
        in_specs=[vmem],
        out_specs=hbm,
        scratch_shapes=[pltpu.VMEM((SHARE // 16, 16, GROUP, GRID), BF16), dma((SHARE // 16,))],
        compiler_params=pltpu.CompilerParams(vmem_limit_bytes=20 * 2**20),
        cost_estimate=pl.CostEstimate(flops=10**9, bytes_accessed=8 * 2**20, transcendentals=0),
    )(moved)
    return out[:, :, None, :]


def solution(mesh):
    return jax.shard_map(
        local,
        mesh=mesh,
        in_specs=(
            P("mem", None, "reg", None),
            P("mem", "reg", None, None),
            P("mem", "reg", None),
            P("mem", "reg", None),
            P("mem", "reg", None),
            P("mem", "reg", None),
            P("mem", "reg"),
            P("mem", "reg", None),
        ),
        out_specs=P("mem", None, "reg", None),
        check_vma=False,
    )
```

```python
import functools

import jax
import jax.numpy as jnp
from jax import lax
from jax.experimental import pallas as pl
from jax.experimental.pallas import tpu as pltpu
from jax.sharding import PartitionSpec as P

MESH = pl.DeviceIdType.MESH
F32, BF16 = jnp.float32, jnp.bfloat16

MEMBERS = 1024
OWN = 2048
RIM = 512
WINDOW = OWN + 2 * RIM
LIST = 2560
GROUP = 16
SHARE = MEMBERS // GROUP
GRID = 1920
PARTS = 5
WIDE = GRID // PARTS
RIDGE = (MEMBERS - 1) / 1.1

PEERS = (
    (0, 1), (1, 0), (0, 3), (3, 0),
    (1, 1), (3, 3), (1, 3), (3, 1),
    (0, 2), (2, 0),
    (1, 2), (2, 1), (3, 2), (2, 3),
    (2, 2),
)
NPEER = len(PEERS)
FEW = 15

MID = 0.5
A0 = (36 - 39 * MID + 27 * MID**2 - 9 * MID**3 + MID**4) / 16
A1 = (-39 + 54 * MID - 27 * MID**2 + 4 * MID**3) / 16
A2 = (27 - 27 * MID + 6 * MID**2) / 16
A3 = (-9 + 4 * MID) / 16
A4 = 1 / 16


def dot(left, right):
    return jnp.dot(left, right, preferred_element_type=F32)


def split(value):
    high = value.astype(BF16)
    return high, (value - high.astype(F32)).astype(BF16)


def transpose_perm():
    to = lax.broadcasted_iota(jnp.int32, (256, 256), 0)
    source = lax.broadcasted_iota(jnp.int32, (256, 256), 1)
    return jnp.where((to % 16) * 16 + to // 16 == source, 1.0, 0.0).astype(BF16)


def total(value):
    return jnp.sum(value, axis=(0, 1), keepdims=True)


def eye_tile(row, col, rows, cols):
    return (row + lax.broadcasted_iota(jnp.int32, (rows, cols), 0)) == (
        col + lax.broadcasted_iota(jnp.int32, (rows, cols), 1)
    )


def row_times(mat, row, out):
    def body(c, norm):
        rows = pl.ds(pl.multiple_of(c * 128, 128), 128)
        acc = mat[rows, 0:128] * row[:, 0:128]
        for j in range(1, 8):
            acc += mat[rows, 128 * j : 128 * j + 128] * row[:, 128 * j : 128 * j + 128]
        col = jnp.sum(acc, axis=1, keepdims=True)
        out[rows, :] = jnp.broadcast_to(col, (128, 128))
        return norm + jnp.sum(col * col, axis=0, keepdims=True)

    return lax.fori_loop(0, 8, body, jnp.zeros((1, 1), F32))


def to_column(row, out):
    for c in range(8):
        cols = slice(128 * c, 128 * c + 128)
        out[cols, :] = jnp.broadcast_to(row[:, cols], (128, 128)).T


def col_times(mat, col):
    def body(c, acc):
        rows = pl.ds(pl.multiple_of(c * 128, 128), 128)
        x = col[rows, :]
        return tuple(
            acc[j] + jnp.sum((mat[rows, 128 * j : 128 * j + 128] * x).reshape(16, 8, 128), axis=0)
            for j in range(8)
        )

    acc = lax.fori_loop(0, 8, body, tuple(jnp.zeros((8, 128), F32) for _ in range(8)))
    return jnp.concatenate([jnp.sum(t, axis=0, keepdims=True) for t in acc], axis=1)


def kernel(
    prior, obs, dep_hbm, prec_hbm, code_hbm, position_hbm, tally, local_hbm,
    out,
    dep, prec, code, position, local, stage, send, recv, window, turned, scaled, gram, root, trans, dev, hop, hop_two,
    listed, weight, innov, column, force, rim_out, rim_in, center,
    vector_sem, load_sem, own_sem, obs_sem, hop_sem, rim_ss, rim_rs, vec_ss, vec_rs,
    one_ss, one_rs, two_ss, two_rs, three_ss, three_rs, fs, fr, bs, br, back_sem,
):
    a, b = lax.axis_index("mem"), lax.axis_index("reg")
    y, x = a // 4, a % 4
    plane, odd = b // 2, b % 2
    first_reg, last_reg = b == 0, b == 7

    def peer(k):
        dy, dx = PEERS[k]
        return (((y + dy) % 4) * 4 + (x + dx) % 4, b)

    after = ((a + (b + 1) // 8) % GROUP, (b + 1) % 8)
    before = ((a + 15 + (b + 7) // 8) % GROUP, (b + 7) % 8)
    partner = ((a + 15 + 2 * odd) % GROUP, b + 1 - 2 * odd)

    def remote(src, dst, send_sem, recv_sem, to):
        return pltpu.make_async_remote_copy(
            src_ref=src, dst_ref=dst, send_sem=send_sem, recv_sem=recv_sem,
            device_id=to, device_id_type=MESH,
        )

    def lanes(c):
        return pl.ds(pl.multiple_of(c * WIDE, 128), WIDE)

    def load(c):
        return pltpu.make_async_copy(prior.at[:, :, lanes(c)], stage.at[c], load_sem.at[c])

    def member_rows(d):
        return pl.ds(pl.multiple_of(d * SHARE, SHARE), SHARE)

    def forward(c, k):
        to = peer(k)
        return remote(
            send.at[c, member_rows(to[0]), :], recv.at[c, member_rows(a), :],
            fs.at[c, k], fr.at[c, k], to,
        )

    def forward_own(c):
        return pltpu.make_async_copy(
            send.at[c, member_rows(a), :], recv.at[c, member_rows(a), :], own_sem.at[c]
        )

    def backward(c, k):
        to = peer(k)
        return remote(
            send.at[c, member_rows(to[0]), :], out.at[a, :, lanes(c)], bs.at[c, k], br.at[c, k], to
        )

    def backward_own(c):
        return pltpu.make_async_copy(
            send.at[c, member_rows(a), :], out.at[a, :, lanes(c)], back_sem.at[c]
        )

    barrier = pltpu.get_barrier_semaphore()

    def greet(to):
        pl.semaphore_signal(barrier, inc=1, device_id=to, device_id_type=MESH)

    for k in range(NPEER):
        greet(peer(k))
    for k in range(1, 8):
        greet((a, (b + k) % 8))
    greet(partner)
    pl.when(first_reg)(lambda: greet(before))
    pl.when(last_reg)(lambda: greet(after))

    for c in range(PARTS):
        load(c).start()
    own_rows = pltpu.make_async_copy(obs, window.at[pl.ds(0, OWN), :], obs_sem)
    own_rows.start()
    own_piece = {
        r: pltpu.make_async_copy(obs.at[pl.ds(at, 128), :], hop, hop_sem)
        for r, at in ((0, 0), (7, OWN - 128))
    }
    for r in (0, 7):
        pl.when(b == r)(own_piece[r].start)

    vectors = [
        pltpu.make_async_copy(source, target, vector_sem.at[n])
        for n, (source, target) in enumerate((
            (dep_hbm, dep), (prec_hbm, prec), (code_hbm, code),
            (position_hbm, position), (local_hbm, local),
        ))
    ]
    for copy in vectors:
        copy.start()

    perm = transpose_perm()

    def arrange(c, _):
        load(c).wait()

        def shuffle(g, _):
            rows = pl.ds(pl.multiple_of(g * 16, 16), 16)
            moved = dot(perm, stage[c, rows, :, :].reshape(256, WIDE)).astype(BF16)
            for i in range(16):
                to_rows = pl.ds(pl.multiple_of(i * SHARE + g * 16, 16), 16)
                send[c, to_rows, :] = moved[16 * i : 16 * i + 16, :]
            return _

        return lax.fori_loop(0, SHARE // 16, shuffle, _)

    arrange(0, 0)

    @pl.when(b % 7 != 0)
    def wait_inner():
        pl.semaphore_wait(barrier, NPEER + 8)

    @pl.when(b % 7 == 0)
    def wait_end():
        pl.semaphore_wait(barrier, NPEER + 9)

    small = [
        remote(rim_out.at[side], rim_in.at[1 - side], vec_ss.at[side], vec_rs.at[side], to)
        for side, to in ((0, before), (1, after))
    ]
    large = [
        remote(
            obs.at[pl.ds(at, RIM), :], window.at[pl.ds(OWN + RIM * (1 - side), RIM), :],
            rim_ss.at[side], rim_rs.at[side], (a, to),
        )
        for side, at, to in ((0, 0, (b + 7) % 8), (1, OWN - RIM, (b + 1) % 8))
    ]
    step_one = {
        r: [
            remote(obs.at[pl.ds(at + 128 * q, 128), :], hop, one_ss.at[n], one_rs, (a, 2 * q + r // 7))
            for n, q in enumerate(pieces)
        ]
        for r, at, pieces in ((0, 0, (1, 2, 3)), (7, OWN - RIM, (0, 1, 2)))
    }
    step_two = remote(hop, hop_two, two_ss, two_rs, partner)
    piece_rows = pl.ds(pl.multiple_of(OWN + RIM * odd + 128 * plane, 128), 128)
    step_three = remote(
        hop_two, window.at[piece_rows, :], three_ss, three_rs.at[plane], (a, 7 * odd)
    )
    last_step = {
        r: [
            remote(
                hop_two, window.at[pl.ds(at + 128 * q, 128), :], three_ss, three_rs.at[q], (a, r)
            )
            for q in pieces
        ]
        for r, at, pieces in ((0, OWN, (1, 2, 3)), (7, OWN + RIM, (0, 1, 2)))
    }

    for r in (0, 7):
        pl.when(b == r)(lambda r=r: [copy.start() for copy in step_one[r]] and None)
    for k in range(FEW):
        forward(0, k).start()
    forward_own(0).start()

    pl.when(odd == 1)(large[0].start)
    pl.when(odd == 0)(large[1].start)

    for copy in vectors:
        copy.wait()
    weight[...] = jnp.zeros_like(weight)
    force[...] = jnp.zeros_like(force)
    for h in range(16):
        weight[h : h + 1, :] = prec[:, 128 * h : 128 * h + 128].astype(F32)
        innov[h : h + 1, :] = dep[:, 128 * h : 128 * h + 128].astype(F32)
    for side, first in ((0, 0), (1, 12)):
        rim_out[side, 0:4, :] = weight[first : first + 4, :]
        rim_out[side, 4:8, :] = innov[first : first + 4, :]
    for copy in small:
        copy.start()

    lax.fori_loop(1, PARTS, arrange, 0)
    listed[...] = jnp.zeros_like(listed)
    live = tally[0, 0]

    def place(e, _):
        cols = pl.ds(pl.multiple_of(e * 512, 512), 512)
        entry = e * 512 + lax.broadcasted_iota(jnp.int32, (1, 512), 1)
        which, pos = code[:, cols], position[:, cols]
        row = jnp.where(which == 1, pos, jnp.where(which == 0, pos + RIM, pos + OWN + RIM))
        high, low = row // 128, row % 128
        value = jnp.where(entry < live, local[:, cols], 0.0)
        one = value.astype(BF16).astype(F32)
        two = (value - one).astype(BF16).astype(F32)
        three = value - one - two
        hot_low = (lax.broadcasted_iota(jnp.int32, (128, 512), 0) == low).astype(F32).astype(BF16)
        hot_high = lax.broadcasted_iota(jnp.int32, (32, 512), 0) == high
        for term in (three, two, one):
            part = jnp.where(hot_high, term, 0.0).astype(BF16)
            listed[...] += lax.dot_general(
                part, hot_low, (((1,), (1,)), ((), ())), preferred_element_type=F32
            )
        return _

    lax.fori_loop(0, LIST // 512, place, 0)
    weight[0:16, :] = weight[0:16, :] * listed[0:16, :]

    def send_part(c, _):
        for k in range(NPEER):
            forward(c, k).start()
        forward_own(c).start()
        return _

    for r in (0, 7):
        pl.when(b == r)(own_piece[r].wait)
    pl.when(b % 7 != 0)(step_one[7][0].wait_recv)
    step_two.start()
    pl.when((odd == 0) & (b > 0))(large[0].start)
    pl.when((odd == 1) & (b < 7))(large[1].start)
    for k in range(FEW, NPEER):
        forward(0, k).start()
    lax.fori_loop(1, PARTS, send_part, 0)

    def rows_ready(first, last):
        force_rows = (weight[first:last, :] * innov[first:last, :]).astype(BF16).astype(F32)
        for h in range(first, last):
            force[0:1, 128 * h : 128 * h + 128] = force_rows[h - first : h - first + 1, :]

        def block(h, _):
            rows = pl.ds(pl.multiple_of(h * 128, 128), 128)
            w = jnp.broadcast_to(weight[pl.ds(h, 1), :], (128, 128)).T
            for j in range(8):
                cols = slice(128 * j, 128 * j + 128)
                tile = window[rows, cols]
                scaled[rows, cols] = (tile.astype(F32) * w).astype(BF16)
                turned[cols, rows] = tile.T
            return _

        lax.fori_loop(first, last, block, 0)

    def halves(body):
        def step(t, _):
            n = pl.multiple_of(t * 512, 512)
            body(n, pl.ds(n, 512))
            return _

        lax.fori_loop(0, 2, step, 0)

    def tiles(body):
        def step(t, _):
            m = pl.multiple_of(t * 128, 128)
            body(m, pl.ds(m, 128))
            return _

        lax.fori_loop(0, 8, step, 0)

    own_rows.wait()
    rows_ready(0, 16)


    def gram_own(n, cols):
        gram[:, cols] = dot(turned[:, 0:OWN], scaled[0:OWN, cols])

    halves(gram_own)
    drive = dot(force[:, 0:OWN].astype(BF16), window[0:OWN, :])

    step_two.wait()

    @pl.when(b % 7 != 0)
    def pass_on():
        step_three.start()

    @pl.when(b % 7 == 0)
    def keep():
        window[piece_rows, :] = hop_two[...]

    for copy in small:
        copy.wait()
    pl.when(b < 7)(large[0].wait_recv)
    pl.when(b > 0)(large[1].wait_recv)
    for r in (0, 7):
        pl.when(b == r)(lambda r=r: [copy.wait_recv() for copy in last_step[r]] and None)
    for side in range(2):
        at = slice(16 + 4 * side, 20 + 4 * side)
        weight[at, :] = rim_in[side, 0:4, :] * listed[at, :]
        innov[at, :] = rim_in[side, 4:8, :]
    rows_ready(16, 24)

    high, low, square_bf = (turned.at[:, 1024 * k : 1024 * k + 1024] for k in range(3))
    cubic_bf = scaled.at[0:1024, :]

    def gram_rim(n, cols):
        ridge = jnp.where(eye_tile(0, n, 1024, 512), F32(RIDGE), 0.0)
        system = gram[:, cols] + dot(turned[:, OWN:WINDOW], scaled[OWN:WINDOW, cols]) + ridge
        gram[:, cols] = system
        high[:, cols], low[:, cols] = split(system)

    halves(gram_rim)
    drive += dot(force[:, OWN:WINDOW].astype(BF16), window[OWN:WINDOW, :])

    def square(n, cols):
        root[:, cols] = dot(high[...], low[:, cols]) + dot(low[...], high[:, cols])
        root[:, cols] += dot(high[...], high[:, cols])

    halves(square)

    norm = row_times(root, jnp.ones((1, MEMBERS), F32), column)
    column[...] = column[...] / jnp.sqrt(norm)
    row = col_times(root, column)
    row = row / jnp.sqrt(total(row * row))
    norm = row_times(root, row, column)
    column[...] = column[...] / jnp.sqrt(norm)
    probe = jnp.concatenate(
        [column[128 * c : 128 * c + 128, :].T[0:1, :] for c in range(8)], axis=1
    )
    bound = total(probe * col_times(gram, column))
    inverse = 1.0 / bound

    def factors(m, rows):
        diagonal = eye_tile(m, 0, 128, 1024)
        unit = gram[rows, :] * inverse
        v = unit - jnp.where(diagonal, F32(MID), 0.0)
        s = root[rows, :] * (inverse * inverse) - 2 * MID * unit
        s += jnp.where(diagonal, F32(MID * MID), 0.0)
        square_bf[rows, :] = s.astype(BF16)
        cubic_bf[rows, :] = (A3 * v + A4 * s).astype(BF16)
        root[rows, :] = jnp.where(diagonal, F32(A0), 0.0) + A1 * v + A2 * s

    tiles(factors)

    def quartic(n, cols):
        root[:, cols] += dot(square_bf[...], cubic_bf[:, cols])

    halves(quartic)

    to_column(drive[0:1, :], column)
    to_column(col_times(root, column), column)
    mean = col_times(root, column) * inverse
    size = jnp.sqrt((MEMBERS - 1) * inverse)

    def finish(m, rows):
        trans[rows, :] = (root[rows, :] * size + mean).astype(BF16)

    tiles(finish)

    def apply_part(c, _):
        for k in range(NPEER):
            forward(c, k).wait()
        forward_own(c).wait()

        def add(g, acc):
            rows = pl.ds(pl.multiple_of(g * 128, 128), 128)
            return acc + jnp.sum(recv[c, rows, :].astype(F32).reshape(16, 8, WIDE), axis=0)

        acc = lax.fori_loop(0, 8, add, jnp.zeros((8, WIDE), F32))
        center[...] = jnp.sum(acc, axis=0, keepdims=True) / MEMBERS

        def deviate(g, _):
            rows = pl.ds(pl.multiple_of(g * 128, 128), 128)
            dev[rows, :] = (recv[c, rows, :].astype(F32) - center[...]).astype(BF16)
            return _

        lax.fori_loop(0, 8, deviate, 0)
        send[c] = (center[...] + dot(trans[...], dev[...])).astype(BF16)
        for k in range(NPEER):
            backward(c, k).start()
        backward_own(c).start()
        return _

    lax.fori_loop(0, PARTS, apply_part, 0)

    pl.when(b > 0)(large[0].wait_send)
    pl.when(b < 7)(large[1].wait_send)
    for r in (0, 7):
        pl.when(b == r)(lambda r=r: [copy.wait_send() for copy in step_one[r]] and None)
    pl.when(b % 7 != 0)(step_three.wait_send)

    def drain(c, _):
        for k in range(NPEER):
            backward(c, k).wait()
        backward_own(c).wait()
        return _

    lax.fori_loop(0, PARTS, drain, 0)


def finish_kernel(moved, out, buffer, sem):
    def store(g):
        return pltpu.make_async_copy(buffer.at[g], out.at[pl.ds(16 * g, 16)], sem.at[g])

    perm = transpose_perm()
    for g in range(SHARE // 16):
        rows = moved[:, 16 * g : 16 * g + 16, :].reshape(256, GRID)
        buffer[g] = dot(perm, rows).astype(BF16).reshape(16, 16, GRID)
        store(g).start()
    for g in range(SHARE // 16):
        store(g).wait()


def local(
    prior_samples,
    measured_anomalies,
    measured_departure,
    measure_inverse_variance,
    measure_neighbour_code,
    measure_position,
    measure_tally,
    locality_weights,
):
    hbm = pl.BlockSpec(memory_space=pl.ANY)
    vmem = pl.BlockSpec(memory_space=pltpu.VMEM)
    dma = pltpu.SemaphoreType.DMA
    moved = pl.pallas_call(
        kernel,
        out_shape=pltpu.VMEM((GROUP, SHARE, GRID), BF16),
        in_specs=[hbm] * 6 + [pl.BlockSpec(memory_space=pltpu.SMEM), hbm],
        out_specs=vmem,
        scratch_shapes=[
            pltpu.VMEM((1, OWN), BF16),
            pltpu.VMEM((1, OWN), BF16),
            pltpu.VMEM((1, LIST), jnp.int32),
            pltpu.VMEM((1, LIST), jnp.int32),
            pltpu.VMEM((1, LIST), F32),
            pltpu.VMEM((PARTS, SHARE, GROUP, WIDE), BF16),
            pltpu.VMEM((PARTS, MEMBERS, WIDE), BF16),
            pltpu.VMEM((PARTS, MEMBERS, WIDE), BF16),
            pltpu.VMEM((WINDOW, MEMBERS), BF16),
            pltpu.VMEM((MEMBERS, WINDOW), BF16),
            pltpu.VMEM((WINDOW, MEMBERS), BF16),
            pltpu.VMEM((MEMBERS, MEMBERS), F32),
            pltpu.VMEM((MEMBERS, MEMBERS), F32),
            pltpu.VMEM((MEMBERS, MEMBERS), BF16),
            pltpu.VMEM((MEMBERS, WIDE), BF16),
            pltpu.VMEM((128, MEMBERS), BF16),
            pltpu.VMEM((128, MEMBERS), BF16),
            pltpu.VMEM((32, 128), F32),
            pltpu.VMEM((24, 128), F32),
            pltpu.VMEM((24, 128), F32),
            pltpu.VMEM((MEMBERS, 128), F32),
            pltpu.VMEM((16, WINDOW), F32),
            pltpu.VMEM((2, 8, 128), F32),
            pltpu.VMEM((2, 8, 128), F32),
            pltpu.VMEM((1, WIDE), F32),
            dma((5,)), dma((PARTS,)), dma((PARTS,)), dma, dma,
            dma((2,)), dma((2,)), dma((2,)), dma((2,)),
            dma((3,)), dma, dma, dma, dma, dma((4,)),
            dma((PARTS, NPEER)), dma((PARTS, NPEER)), dma((PARTS, NPEER)), dma((PARTS, NPEER)),
            dma((PARTS,)),
        ],
        compiler_params=pltpu.CompilerParams(
            collective_id=0, has_side_effects=True, vmem_limit_bytes=54 * 2**20
        ),
        cost_estimate=pl.CostEstimate(flops=24 * 10**9, bytes_accessed=12 * 2**20, transcendentals=0),
    )(
        prior_samples[:, :, 0, :],
        measured_anomalies[0, 0],
        measured_departure[0],
        measure_inverse_variance[0],
        measure_neighbour_code[0],
        measure_position[0],
        measure_tally,
        locality_weights[0],
    )
    out = pl.pallas_call(
        finish_kernel,
        out_shape=jax.ShapeDtypeStruct((SHARE, GROUP, GRID), BF16),
        in_specs=[vmem],
        out_specs=hbm,
        scratch_shapes=[pltpu.VMEM((SHARE // 16, 16, GROUP, GRID), BF16), dma((SHARE // 16,))],
        compiler_params=pltpu.CompilerParams(vmem_limit_bytes=20 * 2**20),
        cost_estimate=pl.CostEstimate(flops=10**9, bytes_accessed=8 * 2**20, transcendentals=0),
    )(moved)
    return out[:, :, None, :]


def solution(mesh):
    return jax.shard_map(
        local,
        mesh=mesh,
        in_specs=(
            P("mem", None, "reg", None),
            P("mem", "reg", None, None),
            P("mem", "reg", None),
            P("mem", "reg", None),
            P("mem", "reg", None),
            P("mem", "reg", None),
            P("mem", "reg"),
            P("mem", "reg", None),
        ),
        out_specs=P("mem", None, "reg", None),
        check_vma=False,
    )
```

```python
import functools

import jax
import jax.numpy as jnp
from jax import lax
from jax.experimental import pallas as pl
from jax.experimental.pallas import tpu as pltpu
from jax.sharding import PartitionSpec as P

MESH = pl.DeviceIdType.MESH
F32, BF16 = jnp.float32, jnp.bfloat16

MEMBERS = 1024
OWN = 2048
RIM = 512
WINDOW = OWN + 2 * RIM
LIST = 2560
GROUP = 16
SHARE = MEMBERS // GROUP
GRID = 1920
PARTS = 5
WIDE = GRID // PARTS
RIDGE = (MEMBERS - 1) / 1.1

PEERS = (
    (0, 1), (1, 0), (0, 3), (3, 0),
    (1, 1), (3, 3), (1, 3), (3, 1),
    (0, 2), (2, 0),
    (1, 2), (2, 1), (3, 2), (2, 3),
    (2, 2),
)
NPEER = len(PEERS)
FEW = 15

MID = 0.5
A0 = (36 - 39 * MID + 27 * MID**2 - 9 * MID**3 + MID**4) / 16
A1 = (-39 + 54 * MID - 27 * MID**2 + 4 * MID**3) / 16
A2 = (27 - 27 * MID + 6 * MID**2) / 16
A3 = (-9 + 4 * MID) / 16
A4 = 1 / 16


def dot(left, right):
    return jnp.dot(left, right, preferred_element_type=F32)


def split(value):
    high = value.astype(BF16)
    return high, (value - high.astype(F32)).astype(BF16)


def transpose_perm():
    to = lax.broadcasted_iota(jnp.int32, (256, 256), 0)
    source = lax.broadcasted_iota(jnp.int32, (256, 256), 1)
    return jnp.where((to % 16) * 16 + to // 16 == source, 1.0, 0.0).astype(BF16)


def total(value):
    return jnp.sum(value, axis=(0, 1), keepdims=True)


def eye_tile(row, col, rows, cols):
    return (row + lax.broadcasted_iota(jnp.int32, (rows, cols), 0)) == (
        col + lax.broadcasted_iota(jnp.int32, (rows, cols), 1)
    )


def row_times(mat, row, out):
    def body(c, norm):
        rows = pl.ds(pl.multiple_of(c * 128, 128), 128)
        acc = mat[rows, 0:128] * row[:, 0:128]
        for j in range(1, 8):
            acc += mat[rows, 128 * j : 128 * j + 128] * row[:, 128 * j : 128 * j + 128]
        col = jnp.sum(acc, axis=1, keepdims=True)
        out[rows, :] = jnp.broadcast_to(col, (128, 128))
        return norm + jnp.sum(col * col, axis=0, keepdims=True)

    return lax.fori_loop(0, 8, body, jnp.zeros((1, 1), F32))


def to_column(row, out):
    for c in range(8):
        cols = slice(128 * c, 128 * c + 128)
        out[cols, :] = jnp.broadcast_to(row[:, cols], (128, 128)).T


def col_times(mat, col):
    def body(c, acc):
        rows = pl.ds(pl.multiple_of(c * 128, 128), 128)
        x = col[rows, :]
        return tuple(
            acc[j] + jnp.sum((mat[rows, 128 * j : 128 * j + 128] * x).reshape(16, 8, 128), axis=0)
            for j in range(8)
        )

    acc = lax.fori_loop(0, 8, body, tuple(jnp.zeros((8, 128), F32) for _ in range(8)))
    return jnp.concatenate([jnp.sum(t, axis=0, keepdims=True) for t in acc], axis=1)


def kernel(
    prior, obs, dep_hbm, prec_hbm, code_hbm, position_hbm, tally, local_hbm,
    out,
    dep, prec, code, position, local, stage, send, recv, window, turned, scaled, gram, root, trans, dev, hop, hop_two,
    listed, weight, innov, column, force, rim_out, rim_in, center,
    vector_sem, load_sem, own_sem, obs_sem, hop_sem, rim_ss, rim_rs, vec_ss, vec_rs,
    one_ss, one_rs, two_ss, two_rs, three_ss, three_rs, fs, fr, bs, br, back_sem,
):
    a, b = lax.axis_index("mem"), lax.axis_index("reg")
    y, x = a // 4, a % 4
    plane, odd = b // 2, b % 2
    first_reg, last_reg = b == 0, b == 7

    def peer(k):
        dy, dx = PEERS[k]
        return (((y + dy) % 4) * 4 + (x + dx) % 4, b)

    after = ((a + (b + 1) // 8) % GROUP, (b + 1) % 8)
    before = ((a + 15 + (b + 7) // 8) % GROUP, (b + 7) % 8)
    partner = ((a + 15 + 2 * odd) % GROUP, b + 1 - 2 * odd)

    def remote(src, dst, send_sem, recv_sem, to):
        return pltpu.make_async_remote_copy(
            src_ref=src, dst_ref=dst, send_sem=send_sem, recv_sem=recv_sem,
            device_id=to, device_id_type=MESH,
        )

    def lanes(c):
        return pl.ds(pl.multiple_of(c * WIDE, 128), WIDE)

    def load(c):
        return pltpu.make_async_copy(prior.at[:, :, lanes(c)], stage.at[c], load_sem.at[c])

    def member_rows(d):
        return pl.ds(pl.multiple_of(d * SHARE, SHARE), SHARE)

    def forward(c, k):
        to = peer(k)
        return remote(
            send.at[c, member_rows(to[0]), :], recv.at[c, member_rows(a), :],
            fs.at[c, k], fr.at[c, k], to,
        )

    def forward_own(c):
        return pltpu.make_async_copy(
            send.at[c, member_rows(a), :], recv.at[c, member_rows(a), :], own_sem.at[c]
        )

    def backward(c, k):
        to = peer(k)
        return remote(
            send.at[c, member_rows(to[0]), :], out.at[a, :, lanes(c)], bs.at[c, k], br.at[c, k], to
        )

    def backward_own(c):
        return pltpu.make_async_copy(
            send.at[c, member_rows(a), :], out.at[a, :, lanes(c)], back_sem.at[c]
        )

    barrier = pltpu.get_barrier_semaphore()

    def greet(to):
        pl.semaphore_signal(barrier, inc=1, device_id=to, device_id_type=MESH)

    for k in range(NPEER):
        greet(peer(k))
    for k in range(1, 8):
        greet((a, (b + k) % 8))
    greet(partner)
    pl.when(first_reg)(lambda: greet(before))
    pl.when(last_reg)(lambda: greet(after))

    for c in range(PARTS):
        load(c).start()
    own_rows = pltpu.make_async_copy(obs, window.at[pl.ds(0, OWN), :], obs_sem)
    own_rows.start()
    own_piece = {
        r: pltpu.make_async_copy(obs.at[pl.ds(at, 128), :], hop, hop_sem)
        for r, at in ((0, 0), (7, OWN - 128))
    }
    for r in (0, 7):
        pl.when(b == r)(own_piece[r].start)

    vectors = [
        pltpu.make_async_copy(source, target, vector_sem.at[n])
        for n, (source, target) in enumerate((
            (dep_hbm, dep), (prec_hbm, prec), (code_hbm, code),
            (position_hbm, position), (local_hbm, local),
        ))
    ]
    for copy in vectors:
        copy.start()

    perm = transpose_perm()

    def arrange(c, _):
        load(c).wait()

        def shuffle(g, _):
            rows = pl.ds(pl.multiple_of(g * 16, 16), 16)
            moved = dot(perm, stage[c, rows, :, :].reshape(256, WIDE)).astype(BF16)
            for i in range(16):
                to_rows = pl.ds(pl.multiple_of(i * SHARE + g * 16, 16), 16)
                send[c, to_rows, :] = moved[16 * i : 16 * i + 16, :]
            return _

        return lax.fori_loop(0, SHARE // 16, shuffle, _)

    arrange(0, 0)

    @pl.when(b % 7 != 0)
    def wait_inner():
        pl.semaphore_wait(barrier, NPEER + 8)

    @pl.when(b % 7 == 0)
    def wait_end():
        pl.semaphore_wait(barrier, NPEER + 9)

    small = [
        remote(rim_out.at[side], rim_in.at[1 - side], vec_ss.at[side], vec_rs.at[side], to)
        for side, to in ((0, before), (1, after))
    ]
    large = [
        remote(
            obs.at[pl.ds(at, RIM), :], window.at[pl.ds(OWN + RIM * (1 - side), RIM), :],
            rim_ss.at[side], rim_rs.at[side], (a, to),
        )
        for side, at, to in ((0, 0, (b + 7) % 8), (1, OWN - RIM, (b + 1) % 8))
    ]
    step_one = {
        r: [
            remote(obs.at[pl.ds(at + 128 * q, 128), :], hop, one_ss.at[n], one_rs, (a, 2 * q + r // 7))
            for n, q in enumerate(pieces)
        ]
        for r, at, pieces in ((0, 0, (1, 2, 3)), (7, OWN - RIM, (0, 1, 2)))
    }
    step_two = remote(hop, hop_two, two_ss, two_rs, partner)
    piece_rows = pl.ds(pl.multiple_of(OWN + RIM * odd + 128 * plane, 128), 128)
    step_three = remote(
        hop_two, window.at[piece_rows, :], three_ss, three_rs.at[plane], (a, 7 * odd)
    )
    last_step = {
        r: [
            remote(
                hop_two, window.at[pl.ds(at + 128 * q, 128), :], three_ss, three_rs.at[q], (a, r)
            )
            for q in pieces
        ]
        for r, at, pieces in ((0, OWN, (1, 2, 3)), (7, OWN + RIM, (0, 1, 2)))
    }

    for r in (0, 7):
        pl.when(b == r)(lambda r=r: [copy.start() for copy in step_one[r]] and None)
    for k in range(FEW):
        forward(0, k).start()
    forward_own(0).start()

    pl.when(odd == 1)(large[0].start)
    pl.when(odd == 0)(large[1].start)

    for copy in vectors:
        copy.wait()
    weight[...] = jnp.zeros_like(weight)
    force[...] = jnp.zeros_like(force)
    for h in range(16):
        weight[h : h + 1, :] = prec[:, 128 * h : 128 * h + 128].astype(F32)
        innov[h : h + 1, :] = dep[:, 128 * h : 128 * h + 128].astype(F32)
    for side, first in ((0, 0), (1, 12)):
        rim_out[side, 0:4, :] = weight[first : first + 4, :]
        rim_out[side, 4:8, :] = innov[first : first + 4, :]
    for copy in small:
        copy.start()

    lax.fori_loop(1, PARTS, arrange, 0)
    listed[...] = jnp.zeros_like(listed)
    live = tally[0, 0]

    def place(e, _):
        cols = pl.ds(pl.multiple_of(e * 512, 512), 512)
        entry = e * 512 + lax.broadcasted_iota(jnp.int32, (1, 512), 1)
        which, pos = code[:, cols], position[:, cols]
        row = jnp.where(which == 1, pos, jnp.where(which == 0, pos + RIM, pos + OWN + RIM))
        high, low = row // 128, row % 128
        value = jnp.where(entry < live, local[:, cols], 0.0)
        one = value.astype(BF16).astype(F32)
        two = (value - one).astype(BF16).astype(F32)
        three = value - one - two
        hot_low = (lax.broadcasted_iota(jnp.int32, (128, 512), 0) == low).astype(F32).astype(BF16)
        hot_high = lax.broadcasted_iota(jnp.int32, (32, 512), 0) == high
        for term in (three, two, one):
            part = jnp.where(hot_high, term, 0.0).astype(BF16)
            listed[...] += lax.dot_general(
                part, hot_low, (((1,), (1,)), ((), ())), preferred_element_type=F32
            )
        return _

    lax.fori_loop(0, LIST // 512, place, 0)
    weight[0:16, :] = weight[0:16, :] * listed[0:16, :]

    def send_part(c, _):
        for k in range(NPEER):
            forward(c, k).start()
        forward_own(c).start()
        return _

    for r in (0, 7):
        pl.when(b == r)(own_piece[r].wait)
    pl.when(b % 7 != 0)(step_one[7][0].wait_recv)
    step_two.start()
    pl.when((odd == 0) & (b > 0))(large[0].start)
    pl.when((odd == 1) & (b < 7))(large[1].start)
    for k in range(FEW, NPEER):
        forward(0, k).start()
    lax.fori_loop(1, PARTS, send_part, 0)

    def rows_ready(first, last):
        force_rows = (weight[first:last, :] * innov[first:last, :]).astype(BF16).astype(F32)
        for h in range(first, last):
            force[0:1, 128 * h : 128 * h + 128] = force_rows[h - first : h - first + 1, :]

        def block(h, _):
            rows = pl.ds(pl.multiple_of(h * 128, 128), 128)
            w = jnp.broadcast_to(weight[pl.ds(h, 1), :], (128, 128)).T
            for j in range(8):
                cols = slice(128 * j, 128 * j + 128)
                tile = window[rows, cols]
                scaled[rows, cols] = (tile.astype(F32) * w).astype(BF16)
                turned[cols, rows] = tile.T
            return _

        lax.fori_loop(first, last, block, 0)

    def halves(body):
        def step(t, _):
            n = pl.multiple_of(t * 512, 512)
            body(n, pl.ds(n, 512))
            return _

        lax.fori_loop(0, 2, step, 0)

    def tiles(body):
        def step(t, _):
            m = pl.multiple_of(t * 128, 128)
            body(m, pl.ds(m, 128))
            return _

        lax.fori_loop(0, 8, step, 0)

    own_rows.wait()
    rows_ready(0, 16)


    def gram_own(n, cols):
        gram[:, cols] = dot(turned[:, 0:OWN], scaled[0:OWN, cols])

    halves(gram_own)
    drive = dot(force[:, 0:OWN].astype(BF16), window[0:OWN, :])

    step_two.wait()

    @pl.when(b % 7 != 0)
    def pass_on():
        step_three.start()

    @pl.when(b % 7 == 0)
    def keep():
        window[piece_rows, :] = hop_two[...]

    for copy in small:
        copy.wait()
    pl.when(b < 7)(large[0].wait_recv)
    pl.when(b > 0)(large[1].wait_recv)
    for r in (0, 7):
        pl.when(b == r)(lambda r=r: [copy.wait_recv() for copy in last_step[r]] and None)
    for side in range(2):
        at = slice(16 + 4 * side, 20 + 4 * side)
        weight[at, :] = rim_in[side, 0:4, :] * listed[at, :]
        innov[at, :] = rim_in[side, 4:8, :]
    rows_ready(16, 24)

    high, low, square_bf = (turned.at[:, 1024 * k : 1024 * k + 1024] for k in range(3))
    cubic_bf = scaled.at[0:1024, :]

    def gram_rim(n, cols):
        ridge = jnp.where(eye_tile(0, n, 1024, 512), F32(RIDGE), 0.0)
        system = gram[:, cols] + dot(turned[:, OWN:WINDOW], scaled[OWN:WINDOW, cols]) + ridge
        gram[:, cols] = system
        high[:, cols], low[:, cols] = split(system)

    halves(gram_rim)
    drive += dot(force[:, OWN:WINDOW].astype(BF16), window[OWN:WINDOW, :])

    def square(n, cols):
        root[:, cols] = dot(high[...], low[:, cols]) + dot(low[...], high[:, cols])
        root[:, cols] += dot(high[...], high[:, cols])

    halves(square)

    norm = row_times(root, jnp.ones((1, MEMBERS), F32), column)
    column[...] = column[...] / jnp.sqrt(norm)
    row = col_times(root, column)
    row = row / jnp.sqrt(total(row * row))
    norm = row_times(root, row, column)
    column[...] = column[...] / jnp.sqrt(norm)
    probe = jnp.concatenate(
        [column[128 * c : 128 * c + 128, :].T[0:1, :] for c in range(8)], axis=1
    )
    bound = total(probe * col_times(gram, column))
    inverse = 1.0 / bound

    def factors(m, rows):
        diagonal = eye_tile(m, 0, 128, 1024)
        unit = gram[rows, :] * inverse
        v = unit - jnp.where(diagonal, F32(MID), 0.0)
        s = root[rows, :] * (inverse * inverse) - 2 * MID * unit
        s += jnp.where(diagonal, F32(MID * MID), 0.0)
        square_bf[rows, :] = s.astype(BF16)
        cubic_bf[rows, :] = (A3 * v + A4 * s).astype(BF16)
        root[rows, :] = jnp.where(diagonal, F32(A0), 0.0) + A1 * v + A2 * s

    tiles(factors)

    def quartic(n, cols):
        root[:, cols] += dot(square_bf[...], cubic_bf[:, cols])

    halves(quartic)

    to_column(drive[0:1, :], column)
    to_column(col_times(root, column), column)
    mean = col_times(root, column) * inverse
    size = jnp.sqrt((MEMBERS - 1) * inverse)

    def finish(m, rows):
        trans[rows, :] = (root[rows, :] * size + mean).astype(BF16)

    tiles(finish)

    def apply_part(c, _):
        for k in range(NPEER):
            forward(c, k).wait()
        forward_own(c).wait()

        def add(g, acc):
            rows = pl.ds(pl.multiple_of(g * 128, 128), 128)
            return acc + jnp.sum(recv[c, rows, :].astype(F32).reshape(16, 8, WIDE), axis=0)

        acc = lax.fori_loop(0, 8, add, jnp.zeros((8, WIDE), F32))
        center[...] = jnp.sum(acc, axis=0, keepdims=True) / MEMBERS

        def deviate(g, _):
            rows = pl.ds(pl.multiple_of(g * 128, 128), 128)
            dev[rows, :] = (recv[c, rows, :].astype(F32) - center[...]).astype(BF16)
            return _

        lax.fori_loop(0, 8, deviate, 0)
        send[c] = (center[...] + dot(trans[...], dev[...])).astype(BF16)
        for k in (14, 0, 10, 1, 11, 2, 12, 3, 13, 4, 8, 5, 9, 6, 7):
            backward(c, k).start()
        backward_own(c).start()
        return _

    lax.fori_loop(0, PARTS, apply_part, 0)

    pl.when(b > 0)(large[0].wait_send)
    pl.when(b < 7)(large[1].wait_send)
    for r in (0, 7):
        pl.when(b == r)(lambda r=r: [copy.wait_send() for copy in step_one[r]] and None)
    pl.when(b % 7 != 0)(step_three.wait_send)

    def drain(c, _):
        for k in range(NPEER):
            backward(c, k).wait()
        backward_own(c).wait()
        return _

    lax.fori_loop(0, PARTS, drain, 0)


def finish_kernel(moved, out, buffer, sem):
    def store(g):
        return pltpu.make_async_copy(buffer.at[g], out.at[pl.ds(16 * g, 16)], sem.at[g])

    perm = transpose_perm()
    for g in range(SHARE // 16):
        rows = moved[:, 16 * g : 16 * g + 16, :].reshape(256, GRID)
        buffer[g] = dot(perm, rows).astype(BF16).reshape(16, 16, GRID)
        store(g).start()
    for g in range(SHARE // 16):
        store(g).wait()


def local(
    prior_samples,
    measured_anomalies,
    measured_departure,
    measure_inverse_variance,
    measure_neighbour_code,
    measure_position,
    measure_tally,
    locality_weights,
):
    hbm = pl.BlockSpec(memory_space=pl.ANY)
    vmem = pl.BlockSpec(memory_space=pltpu.VMEM)
    dma = pltpu.SemaphoreType.DMA
    moved = pl.pallas_call(
        kernel,
        out_shape=pltpu.VMEM((GROUP, SHARE, GRID), BF16),
        in_specs=[hbm] * 6 + [pl.BlockSpec(memory_space=pltpu.SMEM), hbm],
        out_specs=vmem,
        scratch_shapes=[
            pltpu.VMEM((1, OWN), BF16),
            pltpu.VMEM((1, OWN), BF16),
            pltpu.VMEM((1, LIST), jnp.int32),
            pltpu.VMEM((1, LIST), jnp.int32),
            pltpu.VMEM((1, LIST), F32),
            pltpu.VMEM((PARTS, SHARE, GROUP, WIDE), BF16),
            pltpu.VMEM((PARTS, MEMBERS, WIDE), BF16),
            pltpu.VMEM((PARTS, MEMBERS, WIDE), BF16),
            pltpu.VMEM((WINDOW, MEMBERS), BF16),
            pltpu.VMEM((MEMBERS, WINDOW), BF16),
            pltpu.VMEM((WINDOW, MEMBERS), BF16),
            pltpu.VMEM((MEMBERS, MEMBERS), F32),
            pltpu.VMEM((MEMBERS, MEMBERS), F32),
            pltpu.VMEM((MEMBERS, MEMBERS), BF16),
            pltpu.VMEM((MEMBERS, WIDE), BF16),
            pltpu.VMEM((128, MEMBERS), BF16),
            pltpu.VMEM((128, MEMBERS), BF16),
            pltpu.VMEM((32, 128), F32),
            pltpu.VMEM((24, 128), F32),
            pltpu.VMEM((24, 128), F32),
            pltpu.VMEM((MEMBERS, 128), F32),
            pltpu.VMEM((16, WINDOW), F32),
            pltpu.VMEM((2, 8, 128), F32),
            pltpu.VMEM((2, 8, 128), F32),
            pltpu.VMEM((1, WIDE), F32),
            dma((5,)), dma((PARTS,)), dma((PARTS,)), dma, dma,
            dma((2,)), dma((2,)), dma((2,)), dma((2,)),
            dma((3,)), dma, dma, dma, dma, dma((4,)),
            dma((PARTS, NPEER)), dma((PARTS, NPEER)), dma((PARTS, NPEER)), dma((PARTS, NPEER)),
            dma((PARTS,)),
        ],
        compiler_params=pltpu.CompilerParams(
            collective_id=0, has_side_effects=True, vmem_limit_bytes=54 * 2**20
        ),
        cost_estimate=pl.CostEstimate(flops=24 * 10**9, bytes_accessed=12 * 2**20, transcendentals=0),
    )(
        prior_samples[:, :, 0, :],
        measured_anomalies[0, 0],
        measured_departure[0],
        measure_inverse_variance[0],
        measure_neighbour_code[0],
        measure_position[0],
        measure_tally,
        locality_weights[0],
    )
    out = pl.pallas_call(
        finish_kernel,
        out_shape=jax.ShapeDtypeStruct((SHARE, GROUP, GRID), BF16),
        in_specs=[vmem],
        out_specs=hbm,
        scratch_shapes=[pltpu.VMEM((SHARE // 16, 16, GROUP, GRID), BF16), dma((SHARE // 16,))],
        compiler_params=pltpu.CompilerParams(vmem_limit_bytes=20 * 2**20),
        cost_estimate=pl.CostEstimate(flops=10**9, bytes_accessed=8 * 2**20, transcendentals=0),
    )(moved)
    return out[:, :, None, :]


def solution(mesh):
    return jax.shard_map(
        local,
        mesh=mesh,
        in_specs=(
            P("mem", None, "reg", None),
            P("mem", "reg", None, None),
            P("mem", "reg", None),
            P("mem", "reg", None),
            P("mem", "reg", None),
            P("mem", "reg", None),
            P("mem", "reg"),
            P("mem", "reg", None),
        ),
        out_specs=P("mem", None, "reg", None),
        check_vma=False,
    )
```
